32 devices in a mesh: seq: 8 (over y, x, core), chan: 4 (over z).
Axes of the slice: x: 2, y: 2, z: 4, core: 2. Of those that a mesh axis runs over, the one named last changes fastest.
Arguments:
- doc_ids: int32 [2048], replicated, may hold values from 0 to 3, never falling along the last dimension, each value on 1 to 1024 neighbouring positions
- attn_queries: bfloat16 [2048, 8192], P(('seq', 'chan')), may hold values from -6 to 6
- attn_keys: bfloat16 [2048, 8192], P(('seq', 'chan')), may hold values from -6 to 6
- attn_values: bfloat16 [2048, 8192], P(('seq', 'chan')), may hold values from -6 to 6
- attn_cot: bfloat16 [2048, 8192], P(('seq', 'chan')), may hold values from -6 to 6
Outputs:
- attn_out: bfloat16 [2048, 8192], P('seq', 'chan')
- query_grad: bfloat16 [2048, 8192], P('seq', 'chan')
- key_grad: bfloat16 [2048, 8192], P('seq', 'chan')
- value_grad: bfloat16 [2048, 8192], P('seq', 'chan')
The draws below stay inside these ranges and needn't reach their ends.
Inputs may be any that keep to these rules, and one draw needn't show every extreme that they name: `doc_ids`: documents are runs of equal ids that never fall; each holds 1 to 1024 tokens and one holds exactly 1024.
All inputs are finite; a program needn't handle non-finite values.
Results may differ from the reference program's by a relative error of at most 0.03.
Values may be sent and summed in bfloat16 or wider, within the bound.
No kernel may reach another device: no remote copies, remote signals or barrier semaphores. Data moves between devices by JAX's collectives and lax.ppermute only.
A program may use at most 256 MiB of HBM per device.

```python
import math
import jax
import jax.numpy as jnp
import numpy as np
from jax import lax

HEAD_DIM = 128
HEADS = 64
TOK_DEV = 256
SPAN_SH = 4
DOC_MAX = 1024
TOKENS = 2048
DOCS = 4


def drawn_pair(key):
    first_key = jax.random.fold_in(key, 17)
    second_key = jax.random.fold_in(key, 29)
    total_width = HEADS * HEAD_DIM
    query_part = jnp.clip(jax.random.normal(first_key, (TOKENS, total_width), jnp.float32), -6.0, 6.0)
    key_part = jnp.clip(jax.random.normal(second_key, (TOKENS, total_width), jnp.float32), -6.0, 6.0)
    return (query_part, key_part)


def draw_attn_queries(key, part):
    return drawn_pair(key)[0].astype(jnp.bfloat16)


def draw_attn_keys(key, part):
    return drawn_pair(key)[1].astype(jnp.bfloat16)


def steps_of(rng, shape, cuts, smallest, high):
    gain, own = 1.0, jax.random.fold_in(rng, 6)
    for position, shards_of in cuts:
        heights = jnp.exp(jax.random.uniform(jax.random.fold_in(own, position), (shards_of,), jnp.float32, smallest / len(cuts), high / len(cuts)))
        gain = gain * jnp.repeat(heights, shape[position] // shards_of).reshape([-1 if axis == position else 1 for axis in range(len(shape))])
    return gain


def split_up(count, total, most, slope):
    loads = [(1 << 20) // math.isqrt(rank ** slope) + 1 for rank in range(2, count + 1)]
    spare, given = total - most - (count - 1), [1] * (count - 1)
    while spare > 0:
        free = [i for i in range(count - 1) if given[i] < most]
        whole, remaining = sum([loads[i] for i in free]), spare
        for i in free:
            extra = min(most - given[i], max(1, remaining * loads[i] // whole), spare)
            given[i] = given[i] + extra
            spare = spare - extra
    return np.array([most] + given)


def ragged(key, count, total, bound, slope):
    if count == 2:
        one = jax.random.randint(key, (), max(1, total - bound), min(bound, total - 1) + 1)
        return jnp.stack([one, total - one])
    sizes = jnp.asarray(split_up(count, total, bound, slope), jnp.int32)
    pairs = (count - 1) // 2
    donor, sink = sizes[1:1 + 2 * pairs:2], sizes[2:2 + 2 * pairs:2]
    slack = jnp.minimum(donor - 1, bound - sink)
    shifted = jax.random.randint(jax.random.fold_in(key, 1), (pairs,), 0, 1 << 20) % (slack + 1)
    sizes = sizes.at[1:1 + 2 * pairs:2].set(donor - shifted).at[2:2 + 2 * pairs:2].set(sink + shifted)
    return sizes[jax.random.permutation(jax.random.fold_in(key, 2), count)]


def normal_values(own_key, dims, deviation, bound, shards=(), kind=jnp.bfloat16):
    result = deviation * jax.random.normal(own_key, dims, jnp.float32)
    if shards:
        result = result * steps_of(own_key, dims, shards, -0.22, 0.18)
    return jnp.clip(result, -bound, bound).astype(kind)


def setup_inputs(seed: int = 0) -> dict:
    splits = jax.random.split(jax.random.key(seed), 6)
    return {
        "doc_ids": jnp.searchsorted(jnp.cumsum(ragged(splits[0], DOCS, TOKENS, DOC_MAX, 2)), jnp.arange(TOKENS), side="right").astype(jnp.int32),
        "attn_queries": draw_attn_queries(jax.random.fold_in(splits[5], 71), 0),
        "attn_keys": draw_attn_keys(jax.random.fold_in(splits[5], 71), 0),
        "attn_values": normal_values(splits[3], (TOKENS, HEADS * HEAD_DIM), 1.0, 6.0, ((0, 32),)),
        "attn_cot": normal_values(splits[4], (TOKENS, HEADS * HEAD_DIM), 1.0, 6.0, ((0, 32),)),
    }


NEG = -1.0e30


def attention_all(doc_ids, attn_queries, attn_keys, attn_values, attn_cot):
    reach = SPAN_SH * TOK_DEV
    window = reach + TOK_DEV
    score_scale = HEAD_DIM ** -0.5
    block_total = TOKENS // TOK_DEV
    key_doc = jnp.concatenate([jnp.full((reach,), -1, jnp.int32), doc_ids])
    key_pos = jnp.arange(TOKENS + reach, dtype=jnp.int32) - reach

    def one_head(head_id):
        start = head_id * HEAD_DIM
        query_head = lax.dynamic_slice_in_dim(attn_queries, start, HEAD_DIM, 1)
        cot_head = lax.dynamic_slice_in_dim(attn_cot, start, HEAD_DIM, 1)
        front = jnp.zeros((reach, HEAD_DIM), jnp.bfloat16)
        key_head = jnp.concatenate([front, lax.dynamic_slice_in_dim(attn_keys, start, HEAD_DIM, 1)], 0)
        value_head = jnp.concatenate([front, lax.dynamic_slice_in_dim(attn_values, start, HEAD_DIM, 1)], 0)

        def one_block(carry, block_id):
            grad_keys, grad_values = carry
            first = block_id * TOK_DEV
            query_part = lax.dynamic_slice_in_dim(query_head, first, TOK_DEV, 0)
            cot_part = lax.dynamic_slice_in_dim(cot_head, first, TOK_DEV, 0)
            key_part = lax.dynamic_slice_in_dim(key_head, first, window, 0)
            value_part = lax.dynamic_slice_in_dim(value_head, first, window, 0)
            query_doc = lax.dynamic_slice_in_dim(doc_ids, first, TOK_DEV, 0)
            query_pos = first + jnp.arange(TOK_DEV, dtype=jnp.int32)
            part_doc = lax.dynamic_slice_in_dim(key_doc, first, window, 0)
            part_pos = lax.dynamic_slice_in_dim(key_pos, first, window, 0)
            pair_mask = (part_doc[None, :] == query_doc[:, None]) & (part_pos[None, :] <= query_pos[:, None])
            raw_scores = jnp.dot(query_part, key_part.T, preferred_element_type=jnp.float32) * score_scale
            raw_scores = jnp.where(pair_mask, raw_scores, NEG)
            row_peak = jnp.max(raw_scores, axis=1)
            expo = jnp.exp(raw_scores - row_peak[:, None])
            denominator = jnp.sum(expo, axis=1)
            weight = (expo / denominator[:, None]).astype(jnp.bfloat16)
            out_part = jnp.dot(weight, value_part, preferred_element_type=jnp.float32).astype(jnp.bfloat16)
            dweight = jnp.dot(cot_part, value_part.T, preferred_element_type=jnp.float32)
            rowdot = jnp.sum(weight.astype(jnp.float32) * dweight, axis=1)
            dscore = (weight.astype(jnp.float32) * (dweight - rowdot[:, None])).astype(jnp.bfloat16)
            query_part_grad = (score_scale * jnp.dot(dscore, key_part, preferred_element_type=jnp.float32)).astype(jnp.bfloat16)
            key_term = score_scale * jnp.dot(dscore.T, query_part, preferred_element_type=jnp.float32)
            value_term = jnp.dot(weight.T, cot_part, preferred_element_type=jnp.float32)
            grad_keys = lax.dynamic_update_slice_in_dim(grad_keys, lax.dynamic_slice_in_dim(grad_keys, first, window, 0) + key_term, first, 0)
            grad_values = lax.dynamic_update_slice_in_dim(grad_values, lax.dynamic_slice_in_dim(grad_values, first, window, 0) + value_term, first, 0)
            return (grad_keys, grad_values), (out_part, query_part_grad)

        start_carry = (jnp.zeros((TOKENS + reach, HEAD_DIM), jnp.float32), jnp.zeros((TOKENS + reach, HEAD_DIM), jnp.float32))
        final_carry, block_results = lax.scan(one_block, start_carry, jnp.arange(block_total, dtype=jnp.int32))
        out_head = block_results[0].reshape(TOKENS, HEAD_DIM)
        query_grad_head = block_results[1].reshape(TOKENS, HEAD_DIM)
        key_grad_head = final_carry[0][reach:].astype(jnp.bfloat16)
        value_grad_head = final_carry[1][reach:].astype(jnp.bfloat16)
        return out_head, query_grad_head, key_grad_head, value_grad_head

    results = lax.map(one_head, jnp.arange(HEADS, dtype=jnp.int32))
    merged = [jnp.moveaxis(item, 0, 1).reshape(TOKENS, HEADS * HEAD_DIM) for item in results]
    return merged[0], merged[1], merged[2], merged[3]


def reference(doc_ids, attn_queries, attn_keys, attn_values, attn_cot):
    attn_out, query_grad, key_grad, value_grad = attention_all(doc_ids, attn_queries, attn_keys, attn_values, attn_cot)
    return (attn_out, query_grad, key_grad, value_grad)
```

```python
import functools
import math

import jax
import jax.numpy as jnp
from jax import lax
from jax.experimental import pallas as pl
from jax.experimental.pallas import tpu as pltpu
from jax.sharding import PartitionSpec as P

HEAD_DIM = 128
DOC_MAX = 1024
NEG = -1e30
SCALE = HEAD_DIM ** (-0.5)
EXP_SCALE = SCALE * math.log2(math.e)


def dot_nt(a, b):
    return lax.dot_general(a, b, (((1,), (1,)), ((), ())), preferred_element_type=jnp.float32)


def dot_nn(a, b):
    return lax.dot_general(a, b, (((1,), (0,)), ((), ())), preferred_element_type=jnp.float32)


def dot_tn(a, b):
    return lax.dot_general(a, b, (((0,), (0,)), ((), ())), preferred_element_type=jnp.float32)


def attention_kernel(spans, count_ref, start_ref, in_ref, out_ref, key_acc, value_acc):
    rows = in_ref.shape[2]
    blocks, _, block, _ = out_ref.shape
    group = block // rows
    key_acc[...] = jnp.zeros_like(key_acc)
    value_acc[...] = jnp.zeros_like(value_acc)

    def tokens(which, first, count):
        return in_ref[pl.ds(first * group, count * group), which].reshape(count * block, HEAD_DIM)

    def work(i, span):
        low = i - (span - 1)
        width = span * block
        query = tokens(0, i, 1)
        cot = tokens(3, i, 1)
        key = tokens(1, low, span)
        value = tokens(2, low, span)
        start = start_ref[pl.ds(i * block, block), :] - low * block
        col = lax.broadcasted_iota(jnp.int32, (block, width), 1)
        row = lax.broadcasted_iota(jnp.int32, (block, width), 0) + (span - 1) * block
        allowed = (col >= start) & (col <= row)
        score = jnp.where(allowed, dot_nt(query, key), NEG)
        peak = jnp.max(score, axis=1, keepdims=True)
        expo = jnp.exp2((score - peak) * EXP_SCALE)
        inverse = 1.0 / jnp.sum(expo, axis=1, keepdims=True)
        weight = expo * inverse
        weight_low = weight.astype(jnp.bfloat16)
        mixed = dot_nn(weight_low, value)
        rowdot = jnp.sum(mixed * cot.astype(jnp.float32), axis=1, keepdims=True)
        dscore = (weight * (dot_nt(cot, value) - rowdot)).astype(jnp.bfloat16)
        out_ref[i, 0] = mixed.astype(jnp.bfloat16)
        out_ref[i, 1] = (SCALE * dot_nn(dscore, key)).astype(jnp.bfloat16)
        held = pl.ds(pl.multiple_of(low * block, block), width)
        key_acc[held, :] += dot_tn(dscore, query)
        value_acc[held, :] += dot_tn(weight_low, cot)

    def step(i, carry):
        for span in range(1, spans + 1):
            pl.when(count_ref[i] == span)(functools.partial(work, i, span))
        return carry

    lax.fori_loop(0, blocks, step, 0)

    def finish(i, carry):
        held = pl.ds(pl.multiple_of(i * block, block), block)
        out_ref[i, 2] = (SCALE * key_acc[held, :]).astype(jnp.bfloat16)
        out_ref[i, 3] = value_acc[held, :].astype(jnp.bfloat16)
        return carry

    lax.fori_loop(0, blocks, finish, 0)


def attention(count, start, packed, shards):
    sources, _, rows, _ = packed.shape
    total = sources * rows
    block = total // shards
    spans = min(shards, (DOC_MAX + block - 2) // block + 1)
    pairs = total * block * min(spans, 3)
    return pl.pallas_call(
        functools.partial(attention_kernel, spans),
        out_shape=jax.ShapeDtypeStruct((shards, 4, block, HEAD_DIM), jnp.bfloat16),
        in_specs=[
            pl.BlockSpec(memory_space=pltpu.SMEM),
            pl.BlockSpec(memory_space=pltpu.VMEM),
            pl.BlockSpec(memory_space=pltpu.VMEM),
        ],
        out_specs=pl.BlockSpec(memory_space=pltpu.VMEM),
        scratch_shapes=[
            pltpu.VMEM((total, HEAD_DIM), jnp.float32),
            pltpu.VMEM((total, HEAD_DIM), jnp.float32),
        ],
        compiler_params=pltpu.CompilerParams(vmem_limit_bytes=48 * 1024 * 1024),
        cost_estimate=pl.CostEstimate(
            flops=12 * HEAD_DIM * pairs, bytes_accessed=16 * total * HEAD_DIM, transcendentals=pairs
        ),
    )(count, start, packed)


def on_device(doc_ids, *inputs):
    shards = lax.axis_size("seq")
    chans = lax.axis_size("chan")
    rows, width = inputs[0].shape
    heads = width // HEAD_DIM // chans
    turns = max(1, heads // shards)
    owners = heads // turns
    copies = shards // owners
    block = rows * chans
    start = jnp.sum((doc_ids[None, :] < doc_ids[:, None]).astype(jnp.int32), axis=1)
    count = jnp.arange(shards, dtype=jnp.int32) - start[::block] // block + 1
    start = start[:, None]

    split = [x.reshape(rows, chans, turns, owners, HEAD_DIM) for x in inputs]
    results = []
    for turn in range(turns):
        parts = jnp.stack([x[:, :, turn].transpose(2, 1, 0, 3) for x in split], axis=2)
        parts = jnp.repeat(parts, copies, axis=0) if copies > 1 else parts
        parts = parts.reshape(shards * chans, 4, rows, HEAD_DIM)
        packed = lax.all_to_all(parts, ("seq", "chan"), split_axis=0, concat_axis=0, tiled=True)
        done = attention(count, start, packed, shards)
        results.append(lax.all_to_all(done, "seq", split_axis=0, concat_axis=0, tiled=True)[::copies])
    outs = []
    for which in range(4):
        cols = jnp.stack([x[:, which] for x in results], axis=0)
        outs.append(cols.transpose(2, 0, 1, 3).reshape(block, heads * HEAD_DIM))
    return tuple(outs)


def solution(mesh):
    spread = P(("seq", "chan"), None)
    in_specs = (P(), spread, spread, spread, spread)
    out_specs = (P("seq", "chan"),) * 4
    return jax.shard_map(
        on_device, mesh=mesh, in_specs=in_specs, out_specs=out_specs, check_vma=False
    )
```

```python
import functools
import math

import jax
import jax.numpy as jnp
from jax import lax
from jax.experimental import pallas as pl
from jax.experimental.pallas import tpu as pltpu
from jax.sharding import PartitionSpec as P

HEAD_DIM = 128
DOC_MAX = 1024
NEG = -1e30
SCALE = HEAD_DIM ** (-0.5)
EXP_SCALE = SCALE * math.log2(math.e)


def dot_nt(a, b):
    return lax.dot_general(a, b, (((1,), (1,)), ((), ())), preferred_element_type=jnp.float32)


def dot_nn(a, b):
    return lax.dot_general(a, b, (((1,), (0,)), ((), ())), preferred_element_type=jnp.float32)


def dot_tn(a, b):
    return lax.dot_general(a, b, (((0,), (0,)), ((), ())), preferred_element_type=jnp.float32)


def attention_kernel(spans, peers, count_ref, start_ref, target_ref, in_ref, *refs):
    outs, (out_ref, key_acc, value_acc, sems) = refs[:peers], refs[peers:]
    rows = in_ref.shape[2]
    blocks, _, block, _ = out_ref.shape
    group = block // rows
    key_acc[...] = jnp.zeros_like(key_acc)
    value_acc[...] = jnp.zeros_like(value_acc)

    def tokens(which, first, count):
        return in_ref[pl.ds(first * group, count * group), which].reshape(count * block, HEAD_DIM)

    def work(i, span):
        low = i - (span - 1)
        width = span * block
        query = tokens(0, i, 1)
        cot = tokens(3, i, 1)
        key = tokens(1, low, span)
        value = tokens(2, low, span)
        start = start_ref[pl.ds(i * block, block), :] - low * block
        col = lax.broadcasted_iota(jnp.int32, (block, width), 1)
        row = lax.broadcasted_iota(jnp.int32, (block, width), 0) + (span - 1) * block
        allowed = (col >= start) & (col <= row)
        score = jnp.where(allowed, dot_nt(query, key), NEG)
        peak = jnp.max(score, axis=1, keepdims=True)
        expo = jnp.exp2((score - peak) * EXP_SCALE)
        inverse = 1.0 / jnp.sum(expo, axis=1, keepdims=True)
        weight = expo * inverse
        weight_low = weight.astype(jnp.bfloat16)
        mixed = dot_nn(weight_low, value)
        rowdot = jnp.sum(mixed * cot.astype(jnp.float32), axis=1, keepdims=True)
        dscore = (weight * (dot_nt(cot, value) - rowdot)).astype(jnp.bfloat16)
        out_ref[i, 0] = mixed.astype(jnp.bfloat16)
        out_ref[i, 1] = (SCALE * dot_nn(dscore, key)).astype(jnp.bfloat16)
        held = pl.ds(pl.multiple_of(low * block, block), width)
        key_acc[held, :] += dot_tn(dscore, query)
        value_acc[held, :] += dot_tn(weight_low, cot)

    def step(i, carry):
        for span in range(1, spans + 1):
            pl.when(count_ref[i] == span)(functools.partial(work, i, span))
        return carry

    lax.fori_loop(0, blocks, step, 0)

    def finish(i, carry):
        held = pl.ds(pl.multiple_of(i * block, block), block)
        out_ref[i, 2] = (SCALE * key_acc[held, :]).astype(jnp.bfloat16)
        out_ref[i, 3] = value_acc[held, :].astype(jnp.bfloat16)
        return carry

    lax.fori_loop(0, blocks, finish, 0)
    moves = [
        pltpu.make_async_copy(out_ref.at[target_ref[d]], outs[d], sems.at[d]) for d in range(peers)
    ]
    for move in moves:
        move.start()
    for move in moves:
        move.wait()


def attention(count, start, targets, packed):
    sources, _, rows, _ = packed.shape
    shards = targets.shape[0]
    total = sources * rows
    block = total // shards
    spans = min(shards, (DOC_MAX + block - 2) // block + 1)
    pairs = total * block * min(spans, 3)
    return pl.pallas_call(
        functools.partial(attention_kernel, spans, shards),
        out_shape=[jax.ShapeDtypeStruct((4, block, HEAD_DIM), jnp.bfloat16)] * shards,
        in_specs=[
            pl.BlockSpec(memory_space=pltpu.SMEM),
            pl.BlockSpec(memory_space=pltpu.VMEM),
            pl.BlockSpec(memory_space=pltpu.SMEM),
            pl.BlockSpec(memory_space=pltpu.VMEM),
        ],
        out_specs=[pl.BlockSpec(memory_space=pl.ANY)] * shards,
        scratch_shapes=[
            pltpu.VMEM((shards, 4, block, HEAD_DIM), jnp.bfloat16),
            pltpu.VMEM((total, HEAD_DIM), jnp.float32),
            pltpu.VMEM((total, HEAD_DIM), jnp.float32),
            pltpu.SemaphoreType.DMA((shards,)),
        ],
        compiler_params=pltpu.CompilerParams(vmem_limit_bytes=48 * 1024 * 1024),
        cost_estimate=pl.CostEstimate(
            flops=12 * HEAD_DIM * pairs, bytes_accessed=16 * total * HEAD_DIM, transcendentals=pairs
        ),
    )(count, start, targets, packed)


def pack_kernel(owners, *refs):
    ins, out_ref = refs[:4], refs[4]
    for owner in range(owners):
        for which in range(4):
            out_ref[owner, 0, which] = ins[which][:, owner * HEAD_DIM : (owner + 1) * HEAD_DIM]


def pack(inputs, chans, turns, turn):
    rows, width = inputs[0].shape
    owners = width // HEAD_DIM // chans // turns
    shape = (owners, chans, 4, rows, HEAD_DIM)
    return pl.pallas_call(
        functools.partial(pack_kernel, owners),
        grid=(chans,),
        out_shape=jax.ShapeDtypeStruct(shape, jnp.bfloat16),
        in_specs=[pl.BlockSpec((rows, owners * HEAD_DIM), lambda c: (0, c * turns + turn))] * 4,
        out_specs=pl.BlockSpec((owners, 1, 4, rows, HEAD_DIM), lambda c: (0, c, 0, 0, 0)),
        cost_estimate=pl.CostEstimate(
            flops=0, bytes_accessed=4 * math.prod(shape), transcendentals=0
        ),
    )(*inputs)


def unpack_kernel(count, column_ref, *refs):
    blocks, outs, sems = refs[:count], refs[-5:-1], refs[-1]
    moves = []
    for b in range(count):
        columns = pl.ds(pl.multiple_of(column_ref[b] * HEAD_DIM, HEAD_DIM), HEAD_DIM)
        for which in range(4):
            moves.append(
                pltpu.make_async_copy(
                    blocks[b].at[which], outs[which].at[:, columns], sems.at[b, which]
                )
            )
    for move in moves:
        move.start()
    for move in moves:
        move.wait()


def unpack(blocks, columns, width, held):
    count = len(blocks)
    rows = blocks[0].shape[1]
    anywhere = pl.BlockSpec(memory_space=pl.ANY)
    return pl.pallas_call(
        functools.partial(unpack_kernel, count),
        out_shape=[jax.ShapeDtypeStruct((rows, width), jnp.bfloat16)] * 4,
        in_specs=[pl.BlockSpec(memory_space=pltpu.SMEM)] + [anywhere] * (count + len(held)),
        out_specs=[anywhere] * 4,
        scratch_shapes=[pltpu.SemaphoreType.DMA((count, 4))],
        input_output_aliases={1 + count + i: i for i in range(len(held))},
        cost_estimate=pl.CostEstimate(
            flops=0, bytes_accessed=16 * count * rows * HEAD_DIM, transcendentals=0
        ),
    )(columns, *blocks, *held)


def on_device(doc_ids, *inputs):
    shards = lax.axis_size("seq")
    chans = lax.axis_size("chan")
    rows, width = inputs[0].shape
    heads = width // HEAD_DIM // chans
    turns = max(1, heads // shards)
    owners = heads // turns
    copies = shards // owners
    block = rows * chans
    start = jnp.sum((doc_ids[None, :] < doc_ids[:, None]).astype(jnp.int32), axis=1)
    count = jnp.arange(shards, dtype=jnp.int32) - start[::block] // block + 1
    start = start[:, None]
    peers = jnp.bitwise_xor(lax.axis_index("seq"), jnp.arange(shards, dtype=jnp.int32))

    outs = ()
    for turn in range(turns):
        parts = pack(inputs, chans, turns, turn)
        parts = jnp.repeat(parts, copies, axis=0) if copies > 1 else parts
        parts = parts.reshape(shards * chans, 4, rows, HEAD_DIM)
        packed = lax.all_to_all(parts, ("seq", "chan"), split_axis=0, concat_axis=0, tiled=True)
        blocks = attention(count, start, peers, packed)
        if copies == 1:
            blocks = [blocks[0]] + [
                lax.ppermute(blocks[d], "seq", [(s, s ^ d) for s in range(shards)])
                for d in range(1, shards)
            ]
            columns = peers
        else:
            order = jnp.stack(blocks)[peers]
            order = lax.all_to_all(order, "seq", split_axis=0, concat_axis=0, tiled=True)
            blocks = [order[owner * copies] for owner in range(owners)]
            columns = jnp.arange(owners, dtype=jnp.int32)
        outs = unpack(blocks, columns + turn * owners, heads * HEAD_DIM, outs)
    return tuple(outs)


def solution(mesh):
    spread = P(("seq", "chan"), None)
    in_specs = (P(), spread, spread, spread, spread)
    out_specs = (P("seq", "chan"),) * 4
    return jax.shard_map(
        on_device, mesh=mesh, in_specs=in_specs, out_specs=out_specs, check_vma=False
    )
```

```python
import functools
import math

import jax
import jax.numpy as jnp
from jax import lax
from jax.experimental import pallas as pl
from jax.experimental.pallas import tpu as pltpu
from jax.sharding import PartitionSpec as P

HEAD_DIM = 128
DOC_MAX = 1024
NEG = -1e30
SCALE = HEAD_DIM ** (-0.5)
EXP_SCALE = SCALE * math.log2(math.e)


def dot_nt(a, b):
    return lax.dot_general(a, b, (((1,), (1,)), ((), ())), preferred_element_type=jnp.float32)


def dot_nn(a, b):
    return lax.dot_general(a, b, (((1,), (0,)), ((), ())), preferred_element_type=jnp.float32)


def dot_tn(a, b):
    return lax.dot_general(a, b, (((0,), (0,)), ((), ())), preferred_element_type=jnp.float32)


def attention_kernel(spans, pieces, count_ref, start_ref, target_ref, slot_ref, *refs):
    ins, outs = refs[:pieces], refs[pieces:-6]
    in_ref, out_ref, key_acc, value_acc, load_sems, sems = refs[-6:]
    peers = len(outs)
    blocks, _, block, _ = out_ref.shape
    loads = [
        pltpu.make_async_copy(
            ins[e], in_ref if pieces == 1 else in_ref.at[:, slot_ref[e]], load_sems.at[e]
        )
        for e in range(pieces)
    ]
    for load in loads:
        load.start()
    key_acc[...] = jnp.zeros_like(key_acc)
    value_acc[...] = jnp.zeros_like(value_acc)

    for load in loads:
        load.wait()

    def tokens(which, first, count):
        return in_ref[pl.ds(first, count), :, which].reshape(count * block, HEAD_DIM)

    def work(i, span):
        low = i - (span - 1)
        width = span * block
        query = tokens(0, i, 1)
        cot = tokens(3, i, 1)
        key = tokens(1, low, span)
        value = tokens(2, low, span)
        start = start_ref[pl.ds(i * block, block), :] - low * block
        col = lax.broadcasted_iota(jnp.int32, (block, width), 1)
        row = lax.broadcasted_iota(jnp.int32, (block, width), 0) + (span - 1) * block
        allowed = (col >= start) & (col <= row)
        score = jnp.where(allowed, dot_nt(query, key), NEG)
        peak = jnp.max(score, axis=1, keepdims=True)
        expo = jnp.exp2((score - peak) * EXP_SCALE)
        inverse = 1.0 / jnp.sum(expo, axis=1, keepdims=True)
        weight = expo * inverse
        weight_low = weight.astype(jnp.bfloat16)
        mixed = dot_nn(weight_low, value)
        rowdot = jnp.sum(mixed * cot.astype(jnp.float32), axis=1, keepdims=True)
        dscore = (weight * (dot_nt(cot, value) - rowdot)).astype(jnp.bfloat16)
        out_ref[i, 0] = mixed.astype(jnp.bfloat16)
        out_ref[i, 1] = (SCALE * dot_nn(dscore, key)).astype(jnp.bfloat16)
        held = pl.ds(pl.multiple_of(low * block, block), width)
        key_acc[held, :] += dot_tn(dscore, query)
        value_acc[held, :] += dot_tn(weight_low, cot)

    def step(i, carry):
        for span in range(1, spans + 1):
            pl.when(count_ref[i] == span)(functools.partial(work, i, span))
        return carry

    lax.fori_loop(0, blocks, step, 0)

    def finish(i, carry):
        held = pl.ds(pl.multiple_of(i * block, block), block)
        out_ref[i, 2] = (SCALE * key_acc[held, :]).astype(jnp.bfloat16)
        out_ref[i, 3] = value_acc[held, :].astype(jnp.bfloat16)
        return carry

    lax.fori_loop(0, blocks, finish, 0)
    moves = [
        pltpu.make_async_copy(out_ref.at[target_ref[d]], outs[d], sems.at[d]) for d in range(peers)
    ]
    for move in moves:
        move.start()
    for move in moves:
        move.wait()


def attention(count, start, targets, slots, packed):
    shards, chans = targets.shape[0], slots.shape[0]
    rows = packed[0].shape[-2]
    block = chans * rows
    total = shards * block
    spans = min(shards, (DOC_MAX + block - 2) // block + 1)
    pairs = total * block * min(spans, 3)
    scalars = pl.BlockSpec(memory_space=pltpu.SMEM)
    anywhere = pl.BlockSpec(memory_space=pl.ANY)
    return pl.pallas_call(
        functools.partial(attention_kernel, spans, len(packed)),
        out_shape=[jax.ShapeDtypeStruct((4, block, HEAD_DIM), jnp.bfloat16)] * shards,
        in_specs=[scalars, pl.BlockSpec(memory_space=pltpu.VMEM), scalars, scalars]
        + [anywhere] * len(packed),
        out_specs=[anywhere] * shards,
        scratch_shapes=[
            pltpu.VMEM((shards, chans, 4, rows, HEAD_DIM), jnp.bfloat16),
            pltpu.VMEM((shards, 4, block, HEAD_DIM), jnp.bfloat16),
            pltpu.VMEM((total, HEAD_DIM), jnp.float32),
            pltpu.VMEM((total, HEAD_DIM), jnp.float32),
            pltpu.SemaphoreType.DMA((len(packed),)),
            pltpu.SemaphoreType.DMA((shards,)),
        ],
        compiler_params=pltpu.CompilerParams(vmem_limit_bytes=48 * 1024 * 1024),
        cost_estimate=pl.CostEstimate(
            flops=12 * HEAD_DIM * pairs, bytes_accessed=16 * total * HEAD_DIM, transcendentals=pairs
        ),
    )(count, start, targets, slots, *packed)


def pack_kernel(owners, *refs):
    ins, out_ref = refs[:4], refs[4]
    for owner in range(owners):
        for which in range(4):
            out_ref[owner, 0, which] = ins[which][:, owner * HEAD_DIM : (owner + 1) * HEAD_DIM]


def pack(inputs, chans, turns, turn):
    rows, width = inputs[0].shape
    owners = width // HEAD_DIM // chans // turns
    shape = (owners, chans, 4, rows, HEAD_DIM)
    return pl.pallas_call(
        functools.partial(pack_kernel, owners),
        grid=(chans,),
        out_shape=jax.ShapeDtypeStruct(shape, jnp.bfloat16),
        in_specs=[pl.BlockSpec((rows, owners * HEAD_DIM), lambda c: (0, c * turns + turn))] * 4,
        out_specs=pl.BlockSpec((owners, 1, 4, rows, HEAD_DIM), lambda c: (0, c, 0, 0, 0)),
        cost_estimate=pl.CostEstimate(
            flops=0, bytes_accessed=4 * math.prod(shape), transcendentals=0
        ),
    )(*inputs)


def pack_far_kernel(chan_ref, peer_ref, *refs):
    ins, outs = refs[:4], refs[4:]
    for d, out_ref in enumerate(outs):
        columns = pl.ds(pl.multiple_of(peer_ref[d] * HEAD_DIM, HEAD_DIM), HEAD_DIM)
        for which in range(4):
            out_ref[0, which] = ins[which][:, columns]


def pack_far(inputs, slots, peers, turns, turn):
    rows = inputs[0].shape[0]
    shards, chans = peers.shape[0], slots.shape[0]
    return pl.pallas_call(
        pack_far_kernel,
        out_shape=[jax.ShapeDtypeStruct((chans, 4, rows, HEAD_DIM), jnp.bfloat16)] * shards,
        grid_spec=pltpu.PrefetchScalarGridSpec(
            num_scalar_prefetch=2,
            grid=(chans,),
            in_specs=[
                pl.BlockSpec((rows, shards * HEAD_DIM), lambda e, c, p: (0, c[e] * turns + turn))
            ]
            * 4,
            out_specs=[pl.BlockSpec((1, 4, rows, HEAD_DIM), lambda e, c, p: (e, 0, 0, 0))] * shards,
        ),
        cost_estimate=pl.CostEstimate(
            flops=0, bytes_accessed=16 * shards * chans * rows * HEAD_DIM, transcendentals=0
        ),
    )(slots, peers, *inputs)


def regroup_kernel(shards, chans, peer_ref, *refs):
    ins, outs, sems = refs[:shards], refs[shards:-1], refs[-1]
    moves = [
        pltpu.make_async_copy(ins[d].at[e], outs[e].at[peer_ref[d]], sems.at[d, e])
        for e in range(chans)
        for d in range(shards)
    ]
    for move in moves:
        move.start()
    for move in moves:
        move.wait()


def regroup(blocks, peers):
    shards = len(blocks)
    chans, _, rows, _ = blocks[0].shape
    anywhere = pl.BlockSpec(memory_space=pl.ANY)
    return pl.pallas_call(
        functools.partial(regroup_kernel, shards, chans),
        out_shape=[jax.ShapeDtypeStruct((shards, 4, rows, HEAD_DIM), jnp.bfloat16)] * chans,
        in_specs=[pl.BlockSpec(memory_space=pltpu.SMEM)] + [anywhere] * shards,
        out_specs=[anywhere] * chans,
        scratch_shapes=[pltpu.SemaphoreType.DMA((shards, chans))],
        cost_estimate=pl.CostEstimate(
            flops=0, bytes_accessed=16 * shards * chans * rows * HEAD_DIM, transcendentals=0
        ),
    )(peers, *blocks)


def unpack_kernel(count, column_ref, *refs):
    blocks, outs = refs[:count], refs[-4:]
    for b in range(count):
        columns = pl.ds(pl.multiple_of(column_ref[b] * HEAD_DIM, HEAD_DIM), HEAD_DIM)
        for which in range(4):
            outs[which][:, columns] = blocks[b][which]


def unpack(blocks, columns, width, turn, held):
    count = len(blocks)
    rows = blocks[0].shape[1]
    step = min(rows, 64)
    return pl.pallas_call(
        functools.partial(unpack_kernel, count),
        grid=(rows // step,),
        out_shape=[jax.ShapeDtypeStruct((rows, width), jnp.bfloat16)] * 4,
        in_specs=[pl.BlockSpec(memory_space=pltpu.SMEM)]
        + [pl.BlockSpec((4, step, HEAD_DIM), lambda i: (0, i, 0))] * count
        + [pl.BlockSpec(memory_space=pl.ANY)] * len(held),
        out_specs=[pl.BlockSpec((step, count * HEAD_DIM), lambda i: (i, turn))] * 4,
        input_output_aliases={1 + count + i: i for i in range(len(held))},
        cost_estimate=pl.CostEstimate(
            flops=0, bytes_accessed=16 * count * rows * HEAD_DIM, transcendentals=0
        ),
    )(columns, *blocks, *held)


def exchange(value, axis, d):
    return lax.ppermute(value, axis, [(i, i ^ d) for i in range(lax.axis_size(axis))])


def after(value, earlier):
    return lax.optimization_barrier((value, earlier))


def on_device(doc_ids, *inputs):
    shards = lax.axis_size("seq")
    chans = lax.axis_size("chan")
    rows, width = inputs[0].shape
    heads = width // HEAD_DIM // chans
    turns = max(1, heads // shards)
    owners = heads // turns
    copies = shards // owners
    block = rows * chans
    start = jnp.sum((doc_ids[None, :] < doc_ids[:, None]).astype(jnp.int32), axis=1)
    count = jnp.arange(shards, dtype=jnp.int32) - start[::block] // block + 1
    start = start[:, None]
    peers = jnp.bitwise_xor(lax.axis_index("seq"), jnp.arange(shards, dtype=jnp.int32))
    slots = jnp.bitwise_xor(lax.axis_index("chan"), jnp.arange(chans, dtype=jnp.int32))

    gathered = []
    for turn in range(turns):
        if turn == 0:
            parts = pack(inputs, chans, turns, turn)
            parts = jnp.repeat(parts, copies, axis=0) if copies > 1 else parts
            parts = parts.reshape(shards * chans, 4, rows, HEAD_DIM)
            whole = lax.all_to_all(parts, ("seq", "chan"), split_axis=0, concat_axis=0, tiled=True)
            gathered.append([whole.reshape(shards, chans, 4, rows, HEAD_DIM)])
        else:
            far = pack_far(inputs, slots, peers, turns, turn)
            far = [far[0]] + [exchange(far[d], "seq", d) for d in range(1, shards)]
            near = regroup(far, peers)
            gathered.append([near[0]] + [exchange(near[e], "chan", e) for e in range(1, chans)])
            gathered[0][0], _ = after(gathered[0][0], near[0])

    outs = ()
    for turn in range(turns):
        blocks = list(attention(count, start, peers, slots, gathered[turn]))
        if copies == 1:
            for d in range(1, shards):
                if turn + 1 < turns and d > 2:
                    blocks[d], blocks[d - 2] = after(blocks[d], blocks[d - 2])
                blocks[d] = exchange(blocks[d], "seq", d)
            columns = peers
        else:
            order = jnp.stack(blocks)[peers]
            order = lax.all_to_all(order, "seq", split_axis=0, concat_axis=0, tiled=True)
            blocks = [order[owner * copies] for owner in range(owners)]
            columns = jnp.arange(owners, dtype=jnp.int32)
        outs = unpack(blocks, columns, heads * HEAD_DIM, turn, outs)
    return tuple(outs)


def solution(mesh):
    spread = P(("seq", "chan"), None)
    in_specs = (P(), spread, spread, spread, spread)
    out_specs = (P("seq", "chan"),) * 4
    return jax.shard_map(
        on_device, mesh=mesh, in_specs=in_specs, out_specs=out_specs, check_vma=False
    )
```

```python
import functools
import math

import jax
import jax.numpy as jnp
from jax import lax
from jax.experimental import pallas as pl
from jax.experimental.pallas import tpu as pltpu
from jax.sharding import PartitionSpec as P

HEAD_DIM = 128
DOC_MAX = 1024
NEG = -1e30
SCALE = HEAD_DIM ** (-0.5)
EXP_SCALE = SCALE * math.log2(math.e)


def dot_nt(a, b):
    return lax.dot_general(a, b, (((1,), (1,)), ((), ())), preferred_element_type=jnp.float32)


def dot_nn(a, b):
    return lax.dot_general(a, b, (((1,), (0,)), ((), ())), preferred_element_type=jnp.float32)


def dot_tn(a, b):
    return lax.dot_general(a, b, (((0,), (0,)), ((), ())), preferred_element_type=jnp.float32)


def attention_kernel(spans, pieces, count_ref, start_ref, target_ref, slot_ref, *refs):
    ins, outs = refs[:pieces], refs[pieces:-6]
    in_ref, out_ref, key_acc, value_acc, load_sems, sems = refs[-6:]
    peers = len(outs)
    blocks, _, block, _ = out_ref.shape
    loads = [
        pltpu.make_async_copy(
            ins[e], in_ref if pieces == 1 else in_ref.at[:, slot_ref[e]], load_sems.at[e]
        )
        for e in range(pieces)
    ]
    for load in loads:
        load.start()
    key_acc[...] = jnp.zeros_like(key_acc)
    value_acc[...] = jnp.zeros_like(value_acc)

    for load in loads:
        load.wait()

    def tokens(which, first, count):
        return in_ref[pl.ds(first, count), :, which].reshape(count * block, HEAD_DIM)

    def work(i, span):
        low = i - (span - 1)
        width = span * block
        query = tokens(0, i, 1)
        cot = tokens(3, i, 1)
        key = tokens(1, low, span)
        value = tokens(2, low, span)
        start = start_ref[pl.ds(i * block, block), :] - low * block
        col = lax.broadcasted_iota(jnp.int32, (block, width), 1)
        row = lax.broadcasted_iota(jnp.int32, (block, width), 0) + (span - 1) * block
        allowed = (col >= start) & (col <= row)
        score = jnp.where(allowed, dot_nt(query, key), NEG)
        peak = jnp.max(score, axis=1, keepdims=True)
        expo = jnp.exp2((score - peak) * EXP_SCALE)
        inverse = 1.0 / jnp.sum(expo, axis=1, keepdims=True)
        weight = expo * inverse
        weight_low = weight.astype(jnp.bfloat16)
        mixed = dot_nn(weight_low, value)
        rowdot = jnp.sum(mixed * cot.astype(jnp.float32), axis=1, keepdims=True)
        dscore = (weight * (dot_nt(cot, value) - rowdot)).astype(jnp.bfloat16)
        out_ref[i, 0] = mixed.astype(jnp.bfloat16)
        out_ref[i, 1] = (SCALE * dot_nn(dscore, key)).astype(jnp.bfloat16)
        held = pl.ds(pl.multiple_of(low * block, block), width)
        key_acc[held, :] += dot_tn(dscore, query)
        value_acc[held, :] += dot_tn(weight_low, cot)

    def step(i, carry):
        for span in range(1, spans + 1):
            pl.when(count_ref[i] == span)(functools.partial(work, i, span))
        return carry

    lax.fori_loop(0, blocks, step, 0)

    def finish(i, carry):
        held = pl.ds(pl.multiple_of(i * block, block), block)
        out_ref[i, 2] = (SCALE * key_acc[held, :]).astype(jnp.bfloat16)
        out_ref[i, 3] = value_acc[held, :].astype(jnp.bfloat16)
        return carry

    lax.fori_loop(0, blocks, finish, 0)
    moves = [
        pltpu.make_async_copy(out_ref.at[target_ref[d]], outs[d], sems.at[d]) for d in range(peers)
    ]
    for move in moves:
        move.start()
    for move in moves:
        move.wait()


def attention(count, start, targets, slots, packed):
    shards, chans = targets.shape[0], slots.shape[0]
    rows = packed[0].shape[-2]
    block = chans * rows
    total = shards * block
    spans = min(shards, (DOC_MAX + block - 2) // block + 1)
    pairs = total * block * min(spans, 3)
    scalars = pl.BlockSpec(memory_space=pltpu.SMEM)
    anywhere = pl.BlockSpec(memory_space=pl.ANY)
    return pl.pallas_call(
        functools.partial(attention_kernel, spans, len(packed)),
        out_shape=[jax.ShapeDtypeStruct((4, block, HEAD_DIM), jnp.bfloat16)] * shards,
        in_specs=[scalars, pl.BlockSpec(memory_space=pltpu.VMEM), scalars, scalars]
        + [anywhere] * len(packed),
        out_specs=[anywhere] * shards,
        scratch_shapes=[
            pltpu.VMEM((shards, chans, 4, rows, HEAD_DIM), jnp.bfloat16),
            pltpu.VMEM((shards, 4, block, HEAD_DIM), jnp.bfloat16),
            pltpu.VMEM((total, HEAD_DIM), jnp.float32),
            pltpu.VMEM((total, HEAD_DIM), jnp.float32),
            pltpu.SemaphoreType.DMA((len(packed),)),
            pltpu.SemaphoreType.DMA((shards,)),
        ],
        compiler_params=pltpu.CompilerParams(vmem_limit_bytes=48 * 1024 * 1024),
        cost_estimate=pl.CostEstimate(
            flops=12 * HEAD_DIM * pairs, bytes_accessed=16 * total * HEAD_DIM, transcendentals=pairs
        ),
    )(count, start, targets, slots, *packed)


def pack_kernel(owners, shards, chan_ref, peer_ref, *refs):
    ins, first_ref, far = refs[:4], refs[4], refs[5:]
    for which in range(4):
        for owner in range(owners):
            first_ref[owner, 0, which] = ins[which][:, owner * HEAD_DIM : (owner + 1) * HEAD_DIM]
        for i, out_ref in enumerate(far):
            head = (1 + i // shards) * owners + peer_ref[i % shards]
            columns = pl.ds(pl.multiple_of(head * HEAD_DIM, HEAD_DIM), HEAD_DIM)
            out_ref[0, which] = ins[which][:, columns]


def pack(inputs, slots, peers, turns):
    rows, width = inputs[0].shape
    shards, chans = peers.shape[0], slots.shape[0]
    owners = width // HEAD_DIM // chans // turns
    far = (turns - 1) * shards
    return pl.pallas_call(
        functools.partial(pack_kernel, owners, shards),
        out_shape=[jax.ShapeDtypeStruct((owners, chans, 4, rows, HEAD_DIM), jnp.bfloat16)]
        + [jax.ShapeDtypeStruct((chans, 4, rows, HEAD_DIM), jnp.bfloat16)] * far,
        grid_spec=pltpu.PrefetchScalarGridSpec(
            num_scalar_prefetch=2,
            grid=(chans,),
            in_specs=[pl.BlockSpec((rows, width // chans), lambda e, c, p: (0, c[e]))] * 4,
            out_specs=[
                pl.BlockSpec((owners, 1, 4, rows, HEAD_DIM), lambda e, c, p: (0, c[e], 0, 0, 0))
            ]
            + [pl.BlockSpec((1, 4, rows, HEAD_DIM), lambda e, c, p: (e, 0, 0, 0))] * far,
        ),
        cost_estimate=pl.CostEstimate(flops=0, bytes_accessed=16 * rows * width, transcendentals=0),
    )(slots, peers, *inputs)


def regroup_kernel(shards, peer_ref, *refs):
    ins, outs = refs[:shards], refs[shards:]
    for d in range(shards):
        for e, out_ref in enumerate(outs):
            out_ref[peer_ref[d], 0] = ins[d][e, 0]


def regroup(blocks, peers):
    shards = len(blocks)
    chans, _, rows, _ = blocks[0].shape
    return pl.pallas_call(
        functools.partial(regroup_kernel, shards),
        grid=(4,),
        out_shape=[jax.ShapeDtypeStruct((shards, 4, rows, HEAD_DIM), jnp.bfloat16)] * chans,
        in_specs=[pl.BlockSpec(memory_space=pltpu.SMEM)]
        + [pl.BlockSpec((chans, 1, rows, HEAD_DIM), lambda i: (0, i, 0, 0))] * shards,
        out_specs=[pl.BlockSpec((shards, 1, rows, HEAD_DIM), lambda i: (0, i, 0, 0))] * chans,
        cost_estimate=pl.CostEstimate(
            flops=0, bytes_accessed=16 * shards * chans * rows * HEAD_DIM, transcendentals=0
        ),
    )(peers, *blocks)


def unpack_kernel(count, column_ref, *refs):
    blocks, outs = refs[:count], refs[-4:]
    for b in range(count):
        columns = pl.ds(pl.multiple_of(column_ref[b] * HEAD_DIM, HEAD_DIM), HEAD_DIM)
        for which in range(4):
            outs[which][:, columns] = blocks[b][which]


def unpack(blocks, columns, width, turn, held):
    count = len(blocks)
    rows = blocks[0].shape[1]
    step = min(rows, 64)
    return pl.pallas_call(
        functools.partial(unpack_kernel, count),
        grid=(rows // step,),
        out_shape=[jax.ShapeDtypeStruct((rows, width), jnp.bfloat16)] * 4,
        in_specs=[pl.BlockSpec(memory_space=pltpu.SMEM)]
        + [pl.BlockSpec((4, step, HEAD_DIM), lambda i: (0, i, 0))] * count
        + [pl.BlockSpec(memory_space=pl.ANY)] * len(held),
        out_specs=[pl.BlockSpec((step, count * HEAD_DIM), lambda i: (i, turn))] * 4,
        input_output_aliases={1 + count + i: i for i in range(len(held))},
        cost_estimate=pl.CostEstimate(
            flops=0, bytes_accessed=16 * count * rows * HEAD_DIM, transcendentals=0
        ),
    )(columns, *blocks, *held)


def exchange(value, axis, d):
    return lax.ppermute(value, axis, [(i, i ^ d) for i in range(lax.axis_size(axis))])


def after(value, earlier):
    return lax.optimization_barrier((value, earlier))


def on_device(doc_ids, *inputs):
    shards = lax.axis_size("seq")
    chans = lax.axis_size("chan")
    rows, width = inputs[0].shape
    heads = width // HEAD_DIM // chans
    turns = max(1, heads // shards)
    owners = heads // turns
    copies = shards // owners
    block = rows * chans
    start = jnp.sum((doc_ids[None, :] < doc_ids[:, None]).astype(jnp.int32), axis=1)
    count = jnp.arange(shards, dtype=jnp.int32) - start[::block] // block + 1
    start = start[:, None]
    peers = jnp.bitwise_xor(lax.axis_index("seq"), jnp.arange(shards, dtype=jnp.int32))
    slots = jnp.bitwise_xor(lax.axis_index("chan"), jnp.arange(chans, dtype=jnp.int32))

    first, *far = pack(inputs, slots, peers, turns)
    first = jnp.repeat(first, copies, axis=0) if copies > 1 else first
    first = first.reshape(shards * chans, 4, rows, HEAD_DIM)
    first = lax.all_to_all(first, ("seq", "chan"), split_axis=0, concat_axis=0, tiled=True)
    gathered = [[first.reshape(shards, chans, 4, rows, HEAD_DIM)]]
    for turn in range(1, turns):
        mine = far[(turn - 1) * shards : turn * shards]
        near = regroup([mine[0]] + [exchange(mine[d], "seq", d) for d in range(1, shards)], peers)
        gathered.append([near[0]] + [exchange(near[e], "chan", e) for e in range(1, chans)])
        gathered[0][0], _ = after(gathered[0][0], near[0])

    outs = ()
    for turn in range(turns):
        blocks = list(attention(count, start, peers, slots, gathered[turn]))
        if copies == 1:
            for d in range(1, shards):
                if turn + 1 < turns and d > 2:
                    blocks[d], blocks[d - 2] = after(blocks[d], blocks[d - 2])
                blocks[d] = exchange(blocks[d], "seq", d)
            columns = peers
        else:
            order = jnp.stack(blocks)[peers]
            order = lax.all_to_all(order, "seq", split_axis=0, concat_axis=0, tiled=True)
            blocks = [order[owner * copies] for owner in range(owners)]
            columns = jnp.arange(owners, dtype=jnp.int32)
        outs = unpack(blocks, columns, heads * HEAD_DIM, turn, outs)
    return tuple(outs)


def solution(mesh):
    spread = P(("seq", "chan"), None)
    in_specs = (P(), spread, spread, spread, spread)
    out_specs = (P("seq", "chan"),) * 4
    return jax.shard_map(
        on_device, mesh=mesh, in_specs=in_specs, out_specs=out_specs, check_vma=False
    )
```

```python
import functools
import math

import jax
import jax.numpy as jnp
from jax import lax
from jax.experimental import pallas as pl
from jax.experimental.pallas import tpu as pltpu
from jax.sharding import PartitionSpec as P

HEAD_DIM = 128
DOC_MAX = 1024
NEG = -1e30
SCALE = HEAD_DIM ** (-0.5)
EXP_SCALE = SCALE * math.log2(math.e)
SCALARS = pl.BlockSpec(memory_space=pltpu.SMEM)
VECTORS = pl.BlockSpec(memory_space=pltpu.VMEM)
ANYWHERE = pl.BlockSpec(memory_space=pl.ANY)


def low_array(*shape):
    return jax.ShapeDtypeStruct(shape, jnp.bfloat16)


def moved(byte_count):
    return pl.CostEstimate(flops=0, bytes_accessed=byte_count, transcendentals=0)


def dot_nt(a, b):
    return lax.dot_general(a, b, (((1,), (1,)), ((), ())), preferred_element_type=jnp.float32)


def dot_nn(a, b):
    return lax.dot_general(a, b, (((1,), (0,)), ((), ())), preferred_element_type=jnp.float32)


def dot_tn(a, b):
    return lax.dot_general(a, b, (((0,), (0,)), ((), ())), preferred_element_type=jnp.float32)


def pack_kernel(group, size, place_ref, *refs):
    query, key, value, cot, out_ref = refs
    core = place_ref[0]
    for chip in range(group):
        for j in range(size):
            columns = slice((chip * size + j) * HEAD_DIM, (chip * size + j + 1) * HEAD_DIM)
            out_ref[2 * chip + core, 0, j, 0] = query[:, columns]
            out_ref[2 * chip + core, 0, j, 1] = cot[:, columns]
            out_ref[2 * chip + 1 - core, 0, j, 0] = key[:, columns]
            out_ref[2 * chip + 1 - core, 0, j, 1] = value[:, columns]


def pack(place, inputs, chans, group, offset, size):
    rows, width = inputs[0].shape
    part = group * size * HEAD_DIM
    per_chan = width // chans // part
    return pl.pallas_call(
        functools.partial(pack_kernel, group, size),
        grid=(chans,),
        out_shape=low_array(2 * group, chans, size, 2, rows, HEAD_DIM),
        in_specs=[SCALARS]
        + [pl.BlockSpec((rows, part), lambda c: (0, c * per_chan + offset // size))] * 4,
        out_specs=pl.BlockSpec(
            (2 * group, 1, size, 2, rows, HEAD_DIM), lambda c: (0, c, 0, 0, 0, 0)
        ),
        cost_estimate=moved(16 * rows * part * chans),
    )(place, *inputs)


def attention_kernel(spans, size, group, *refs):
    count_ref, place_ref, start_ref, mine_ref, other_ref = refs[:5]
    outs, (keep_ref, send_ref) = refs[5 : 5 + group], refs[5 + group : 7 + group]
    pair_ref, key_ref, mixed_ref, key_acc, value_acc, load_sems, sems = refs[7 + group :]
    block = mixed_ref.shape[3]
    core = place_ref[0]
    loads = []
    for j in range(size):
        for m in range(group):
            same, cross = 2 * m + core, 2 * m + 1 - core
            sem = load_sems.at[j, m]
            for k, (source, target) in enumerate(
                (
                    (mine_ref.at[same, :, j], pair_ref.at[j, m]),
                    (mine_ref.at[cross, :, j], key_ref.at[j, cross]),
                    (other_ref.at[same, :, j], key_ref.at[j, same]),
                )
            ):
                loads.append(pltpu.make_async_copy(source, target, sem.at[k]))
    for load in loads:
        load.start()
    key_acc[...] = jnp.zeros_like(key_acc)
    value_acc[...] = jnp.zeros_like(value_acc)
    for load in loads:
        load.wait()

    def work(j, m, span):
        i = 2 * m + core
        low = i - (span - 1)
        width = span * block
        query = pair_ref[j, m, :, 0].reshape(block, HEAD_DIM)
        cot = pair_ref[j, m, :, 1].reshape(block, HEAD_DIM)
        key = key_ref[j, pl.ds(low, span), :, 0].reshape(width, HEAD_DIM)
        value = key_ref[j, pl.ds(low, span), :, 1].reshape(width, HEAD_DIM)
        start = start_ref[pl.ds(pl.multiple_of(i * block, block), block), :] - low * block
        col = lax.broadcasted_iota(jnp.int32, (block, width), 1)
        row = lax.broadcasted_iota(jnp.int32, (block, width), 0) + (span - 1) * block
        allowed = (col >= start) & (col <= row)
        score = jnp.where(allowed, dot_nt(query, key), NEG)
        peak = jnp.max(score, axis=1, keepdims=True)
        expo = jnp.exp2((score - peak) * EXP_SCALE)
        inverse = 1.0 / jnp.sum(expo, axis=1, keepdims=True)
        weight = expo * inverse
        weight_low = weight.astype(jnp.bfloat16)
        mixed = dot_nn(weight_low, value)
        rowdot = jnp.sum(mixed * cot.astype(jnp.float32), axis=1, keepdims=True)
        dscore = (weight * (dot_nt(cot, value) - rowdot)).astype(jnp.bfloat16)
        mixed_ref[m, j, 0] = mixed.astype(jnp.bfloat16)
        mixed_ref[m, j, 1] = (SCALE * dot_nn(dscore, key)).astype(jnp.bfloat16)
        held = pl.ds(pl.multiple_of(low * block, block), width)
        key_acc[j, held, :] += dot_tn(dscore, query)
        value_acc[j, held, :] += dot_tn(weight_low, cot)

    def step(n, carry):
        j, m = n // group, n % group
        for span in range(1, spans + 1):
            pl.when(count_ref[2 * m + core] == span)(functools.partial(work, j, m, span))
        return carry

    lax.fori_loop(0, size * group, step, 0)
    moves = [
        pltpu.make_async_copy(mixed_ref.at[place_ref[1 + d]], outs[d], sems.at[d])
        for d in range(group)
    ]
    for move in moves:
        move.start()

    def finish(n, carry):
        j, m = n // group, n % group
        own = pl.ds(pl.multiple_of((2 * m + core) * block, block), block)
        cross = pl.ds(pl.multiple_of((2 * m + 1 - core) * block, block), block)
        keep_ref[m, j, 0] = SCALE * key_acc[j, own, :]
        keep_ref[m, j, 1] = value_acc[j, own, :]
        send_ref[m, j, 0] = (SCALE * key_acc[j, cross, :]).astype(jnp.bfloat16)
        send_ref[m, j, 1] = value_acc[j, cross, :].astype(jnp.bfloat16)
        return carry

    lax.fori_loop(0, size * group, finish, 0)
    for move in moves:
        move.wait()


def attention(count, place, start, mine, other):
    shards, chans, size, _, rows, _ = mine.shape
    group = shards // 2
    block = chans * rows
    total = shards * block
    spans = min(shards, (DOC_MAX + block - 2) // block + 1)
    pairs = size * group * block * block * min(spans, 3)
    return pl.pallas_call(
        functools.partial(attention_kernel, spans, size, group),
        out_shape=[low_array(size, 2, block, HEAD_DIM)] * group
        + [
            jax.ShapeDtypeStruct((group, size, 2, block, HEAD_DIM), jnp.float32),
            low_array(group, size, 2, block, HEAD_DIM),
        ],
        in_specs=[SCALARS, SCALARS, VECTORS, ANYWHERE, ANYWHERE],
        out_specs=[ANYWHERE] * group + [VECTORS] * 2,
        scratch_shapes=[
            pltpu.VMEM((size, group, chans, 2, rows, HEAD_DIM), jnp.bfloat16),
            pltpu.VMEM((size, shards, chans, 2, rows, HEAD_DIM), jnp.bfloat16),
            pltpu.VMEM((group, size, 2, block, HEAD_DIM), jnp.bfloat16),
            pltpu.VMEM((size, total, HEAD_DIM), jnp.float32),
            pltpu.VMEM((size, total, HEAD_DIM), jnp.float32),
            pltpu.SemaphoreType.DMA((size, group, 3)),
            pltpu.SemaphoreType.DMA((group,)),
        ],
        compiler_params=pltpu.CompilerParams(vmem_limit_bytes=48 * 1024 * 1024),
        cost_estimate=pl.CostEstimate(
            flops=12 * HEAD_DIM * pairs,
            bytes_accessed=10 * size * total * HEAD_DIM,
            transcendentals=pairs,
        ),
    )(count, place, start, mine, other)


def add_kernel(place_ref, keep_ref, other_ref, *outs):
    for d, out_ref in enumerate(outs):
        m = place_ref[1 + d]
        out_ref[...] = (keep_ref[m] + other_ref[m].astype(jnp.float32)).astype(jnp.bfloat16)


def add(place, keep, other):
    group = keep.shape[0]
    return pl.pallas_call(
        add_kernel,
        out_shape=[low_array(*keep.shape[1:])] * group,
        in_specs=[SCALARS, VECTORS, VECTORS],
        out_specs=[VECTORS] * group,
        compiler_params=pltpu.CompilerParams(vmem_limit_bytes=32 * 1024 * 1024),
        cost_estimate=moved(8 * keep.size),
    )(place, keep, other)


def unpack_kernel(group, size, place_ref, *refs):
    mixed, grads, outs = refs[:group], refs[group : 2 * group], refs[-4:]
    for d in range(group):
        for j in range(size):
            head = place_ref[1 + d] * size + j
            columns = pl.ds(pl.multiple_of(head * HEAD_DIM, HEAD_DIM), HEAD_DIM)
            for which in range(2):
                outs[which][:, columns] = mixed[d][j, which]
                outs[2 + which][:, columns] = grads[d][j, which]


def unpack(place, mixed, grads, width, offset, held):
    group = len(mixed)
    size, _, rows, _ = mixed[0].shape
    step = min(rows, 64)
    return pl.pallas_call(
        functools.partial(unpack_kernel, group, size),
        grid=(rows // step,),
        out_shape=[low_array(rows, width)] * 4,
        in_specs=[SCALARS]
        + [pl.BlockSpec((size, 2, step, HEAD_DIM), lambda i: (0, 0, i, 0))] * (2 * group)
        + [ANYWHERE] * len(held),
        out_specs=[pl.BlockSpec((step, group * size * HEAD_DIM), lambda i: (i, offset // size))] * 4,
        input_output_aliases={1 + 2 * group + i: i for i in range(len(held))},
        cost_estimate=moved(16 * group * size * rows * HEAD_DIM),
    )(place, *mixed, *grads, *held)


def exchange(value, d):
    return lax.ppermute(value, "seq", [(s, s ^ d) for s in range(lax.axis_size("seq"))])


def chunk_sizes(count):
    sizes = []
    while count > 1:
        sizes.append(count // 2)
        count -= count // 2
    return sizes + [count]


def on_device(doc_ids, *inputs):
    shards = lax.axis_size("seq")
    chans = lax.axis_size("chan")
    rows, width = inputs[0].shape
    heads = width // HEAD_DIM // chans
    group = shards // 2
    block = rows * chans
    start = jnp.sum((doc_ids[None, :] < doc_ids[:, None]).astype(jnp.int32), axis=1)
    count = jnp.arange(shards, dtype=jnp.int32) - start[::block] // block + 1
    start = start[:, None]
    shard = lax.axis_index("seq")
    chips = jnp.bitwise_xor(shard // 2, jnp.arange(group, dtype=jnp.int32))
    place = jnp.concatenate([(shard % 2)[None].astype(jnp.int32), chips])

    outs = ()
    offset = 0
    for size in chunk_sizes(heads // group):
        parts = pack(place, inputs, chans, group, offset, size)
        parts = parts.reshape(shards * chans, size, 2, rows, HEAD_DIM)
        mine = lax.all_to_all(parts, ("seq", "chan"), split_axis=0, concat_axis=0, tiled=True)
        mine = mine.reshape(shards, chans, size, 2, rows, HEAD_DIM)
        *mixed, keep, send = attention(count, place, start, mine, exchange(mine, 1))
        mixed = [mixed[0]] + [exchange(mixed[d], 2 * d) for d in range(1, group)]
        grads = add(place, keep, exchange(send, 1))
        grads = [grads[0]] + [exchange(grads[d], 2 * d) for d in range(1, group)]
        count, mixed, grads = lax.optimization_barrier((count, mixed, grads))
        outs = unpack(place, mixed, grads, heads * HEAD_DIM, offset, outs)
        offset += size
    return tuple(outs)


def solution(mesh):
    spread = P(("seq", "chan"), None)
    in_specs = (P(), spread, spread, spread, spread)
    out_specs = (P("seq", "chan"),) * 4
    return jax.shard_map(
        on_device, mesh=mesh, in_specs=in_specs, out_specs=out_specs, check_vma=False
    )
```

```python
import functools
import math

import jax
import jax.numpy as jnp
from jax import lax
from jax.experimental import pallas as pl
from jax.experimental.pallas import tpu as pltpu
from jax.sharding import PartitionSpec as P

HEAD_DIM = 128
DOC_MAX = 1024
NEG = -1e30
SCALE = HEAD_DIM ** (-0.5)
EXP_SCALE = SCALE * math.log2(math.e)
SCALARS = pl.BlockSpec(memory_space=pltpu.SMEM)
VECTORS = pl.BlockSpec(memory_space=pltpu.VMEM)
ANYWHERE = pl.BlockSpec(memory_space=pl.ANY)


def low_array(*shape):
    return jax.ShapeDtypeStruct(shape, jnp.bfloat16)


def moved(byte_count):
    return pl.CostEstimate(flops=0, bytes_accessed=byte_count, transcendentals=0)


def dot_nt(a, b):
    return lax.dot_general(a, b, (((1,), (1,)), ((), ())), preferred_element_type=jnp.float32)


def dot_nn(a, b):
    return lax.dot_general(a, b, (((1,), (0,)), ((), ())), preferred_element_type=jnp.float32)


def dot_tn(a, b):
    return lax.dot_general(a, b, (((0,), (0,)), ((), ())), preferred_element_type=jnp.float32)


def pack_kernel(group, size, place_ref, *refs):
    query, key, value, cot, out_ref = refs
    core = place_ref[0]
    for chip in range(group):
        for j in range(size):
            columns = slice((chip * size + j) * HEAD_DIM, (chip * size + j + 1) * HEAD_DIM)
            out_ref[2 * chip + core, 0, j, 0] = query[:, columns]
            out_ref[2 * chip + core, 0, j, 1] = cot[:, columns]
            out_ref[2 * chip + 1 - core, 0, j, 0] = key[:, columns]
            out_ref[2 * chip + 1 - core, 0, j, 1] = value[:, columns]


def pack(place, inputs, chans, group, offset, size):
    rows, width = inputs[0].shape
    part = group * size * HEAD_DIM
    per_chan = width // chans // part
    return pl.pallas_call(
        functools.partial(pack_kernel, group, size),
        grid=(chans,),
        out_shape=low_array(2 * group, chans, size, 2, rows, HEAD_DIM),
        in_specs=[SCALARS]
        + [pl.BlockSpec((rows, part), lambda c: (0, c * per_chan + offset // size))] * 4,
        out_specs=pl.BlockSpec(
            (2 * group, 1, size, 2, rows, HEAD_DIM), lambda c: (0, c, 0, 0, 0, 0)
        ),
        cost_estimate=moved(16 * rows * part * chans),
    )(place, *inputs)


def attention_kernel(spans, size, group, *refs):
    count_ref, place_ref, start_ref, mine_ref, other_ref = refs[:5]
    outs, (keep_ref, send_ref) = refs[5 : 5 + group], refs[5 + group : 7 + group]
    pair_ref, key_ref, mixed_ref, key_acc, value_acc, load_sems, sems = refs[7 + group :]
    block = mixed_ref.shape[3]
    core = place_ref[0]
    loads = []
    for j in range(size):
        for m in range(group):
            same, cross = 2 * m + core, 2 * m + 1 - core
            sem = load_sems.at[j, m]
            for k, (source, target) in enumerate(
                (
                    (mine_ref.at[same, :, j], pair_ref.at[j, m]),
                    (mine_ref.at[cross, :, j], key_ref.at[j, cross]),
                    (other_ref.at[same, :, j], key_ref.at[j, same]),
                )
            ):
                loads.append(pltpu.make_async_copy(source, target, sem.at[k]))
    for load in loads:
        load.start()
    key_acc[...] = jnp.zeros_like(key_acc)
    value_acc[...] = jnp.zeros_like(value_acc)
    for load in loads:
        load.wait()

    def work(j, m, span):
        i = 2 * m + core
        low = i - (span - 1)
        width = span * block
        query = pair_ref[j, m, :, 0].reshape(block, HEAD_DIM)
        cot = pair_ref[j, m, :, 1].reshape(block, HEAD_DIM)
        key = key_ref[j, pl.ds(low, span), :, 0].reshape(width, HEAD_DIM)
        value = key_ref[j, pl.ds(low, span), :, 1].reshape(width, HEAD_DIM)
        start = start_ref[pl.ds(pl.multiple_of(i * block, block), block), :] - low * block
        col = lax.broadcasted_iota(jnp.int32, (block, width), 1)
        row = lax.broadcasted_iota(jnp.int32, (block, width), 0) + (span - 1) * block
        allowed = (col >= start) & (col <= row)
        score = jnp.where(allowed, dot_nt(query, key), NEG)
        peak = jnp.max(score, axis=1, keepdims=True)
        expo = jnp.exp2((score - peak) * EXP_SCALE)
        inverse = 1.0 / jnp.sum(expo, axis=1, keepdims=True)
        weight = expo * inverse
        weight_low = weight.astype(jnp.bfloat16)
        mixed = dot_nn(weight_low, value)
        rowdot = jnp.sum(mixed * cot.astype(jnp.float32), axis=1, keepdims=True)
        dscore = (weight * (dot_nt(cot, value) - rowdot)).astype(jnp.bfloat16)
        mixed_ref[m, j, 0] = mixed.astype(jnp.bfloat16)
        mixed_ref[m, j, 1] = (SCALE * dot_nn(dscore, key)).astype(jnp.bfloat16)
        held = pl.ds(pl.multiple_of(low * block, block), width)
        key_acc[j, held, :] += dot_tn(dscore, query)
        value_acc[j, held, :] += dot_tn(weight_low, cot)

    def step(n, carry):
        j, m = n // group, n % group
        for span in range(1, spans + 1):
            pl.when(count_ref[2 * m + core] == span)(functools.partial(work, j, m, span))
        return carry

    lax.fori_loop(0, size * group, step, 0)
    moves = [
        pltpu.make_async_copy(mixed_ref.at[place_ref[1 + d]], outs[d], sems.at[d])
        for d in range(group)
    ]
    for move in moves:
        move.start()

    def finish(n, carry):
        j, m = n // group, n % group
        own = pl.ds(pl.multiple_of((2 * m + core) * block, block), block)
        cross = pl.ds(pl.multiple_of((2 * m + 1 - core) * block, block), block)
        keep_ref[m, j, 0] = SCALE * key_acc[j, own, :]
        keep_ref[m, j, 1] = value_acc[j, own, :]
        send_ref[m, j, 0] = (SCALE * key_acc[j, cross, :]).astype(jnp.bfloat16)
        send_ref[m, j, 1] = value_acc[j, cross, :].astype(jnp.bfloat16)
        return carry

    lax.fori_loop(0, size * group, finish, 0)
    for move in moves:
        move.wait()


def attention(count, place, start, mine, other):
    shards, chans, size, _, rows, _ = mine.shape
    group = shards // 2
    block = chans * rows
    total = shards * block
    spans = min(shards, (DOC_MAX + block - 2) // block + 1)
    pairs = size * group * block * block * min(spans, 3)
    return pl.pallas_call(
        functools.partial(attention_kernel, spans, size, group),
        out_shape=[low_array(size, 2, block, HEAD_DIM)] * group
        + [
            jax.ShapeDtypeStruct((group, size, 2, block, HEAD_DIM), jnp.float32),
            low_array(group, size, 2, block, HEAD_DIM),
        ],
        in_specs=[SCALARS, SCALARS, VECTORS, ANYWHERE, ANYWHERE],
        out_specs=[ANYWHERE] * group + [VECTORS] * 2,
        scratch_shapes=[
            pltpu.VMEM((size, group, chans, 2, rows, HEAD_DIM), jnp.bfloat16),
            pltpu.VMEM((size, shards, chans, 2, rows, HEAD_DIM), jnp.bfloat16),
            pltpu.VMEM((group, size, 2, block, HEAD_DIM), jnp.bfloat16),
            pltpu.VMEM((size, total, HEAD_DIM), jnp.float32),
            pltpu.VMEM((size, total, HEAD_DIM), jnp.float32),
            pltpu.SemaphoreType.DMA((size, group, 3)),
            pltpu.SemaphoreType.DMA((group,)),
        ],
        compiler_params=pltpu.CompilerParams(vmem_limit_bytes=48 * 1024 * 1024),
        cost_estimate=pl.CostEstimate(
            flops=12 * HEAD_DIM * pairs,
            bytes_accessed=10 * size * total * HEAD_DIM,
            transcendentals=pairs,
        ),
    )(count, place, start, mine, other)


def add_kernel(place_ref, keep_ref, other_ref, *outs):
    for d, out_ref in enumerate(outs):
        m = place_ref[1 + d]
        out_ref[...] = (keep_ref[m] + other_ref[m].astype(jnp.float32)).astype(jnp.bfloat16)


def add(place, keep, other):
    group = keep.shape[0]
    return pl.pallas_call(
        add_kernel,
        out_shape=[low_array(*keep.shape[1:])] * group,
        in_specs=[SCALARS, VECTORS, VECTORS],
        out_specs=[VECTORS] * group,
        compiler_params=pltpu.CompilerParams(vmem_limit_bytes=32 * 1024 * 1024),
        cost_estimate=moved(8 * keep.size),
    )(place, keep, other)


def unpack_kernel(group, size, place_ref, *refs):
    mixed, grads, outs = refs[:group], refs[group : 2 * group], refs[-4:]
    for d in range(group):
        for j in range(size):
            head = place_ref[1 + d] * size + j
            columns = pl.ds(pl.multiple_of(head * HEAD_DIM, HEAD_DIM), HEAD_DIM)
            for which in range(2):
                outs[which][:, columns] = mixed[d][j, which]
                outs[2 + which][:, columns] = grads[d][j, which]


def unpack(place, mixed, grads, width, offset, held):
    group = len(mixed)
    size, _, rows, _ = mixed[0].shape
    step = min(rows, 64)
    return pl.pallas_call(
        functools.partial(unpack_kernel, group, size),
        grid=(rows // step,),
        out_shape=[low_array(rows, width)] * 4,
        in_specs=[SCALARS]
        + [pl.BlockSpec((size, 2, step, HEAD_DIM), lambda i: (0, 0, i, 0))] * (2 * group)
        + [ANYWHERE] * len(held),
        out_specs=[pl.BlockSpec((step, group * size * HEAD_DIM), lambda i: (i, offset // size))] * 4,
        input_output_aliases={1 + 2 * group + i: i for i in range(len(held))},
        cost_estimate=moved(16 * group * size * rows * HEAD_DIM),
    )(place, *mixed, *grads, *held)


def exchange(value, d):
    return lax.ppermute(value, "seq", [(s, s ^ d) for s in range(lax.axis_size("seq"))])


def on_device(doc_ids, *inputs):
    shards = lax.axis_size("seq")
    chans = lax.axis_size("chan")
    rows, width = inputs[0].shape
    heads = width // HEAD_DIM // chans
    group = shards // 2
    block = rows * chans
    start = jnp.sum((doc_ids[None, :] < doc_ids[:, None]).astype(jnp.int32), axis=1)
    count = jnp.arange(shards, dtype=jnp.int32) - start[::block] // block + 1
    start = start[:, None]
    shard = lax.axis_index("seq")
    chips = jnp.bitwise_xor(shard // 2, jnp.arange(group, dtype=jnp.int32))
    place = jnp.concatenate([(shard % 2)[None].astype(jnp.int32), chips])

    gathered = []
    for chunk in range(heads // group):
        parts = pack(place, inputs, chans, group, chunk, 1)
        parts = parts.reshape(shards * chans, 1, 2, rows, HEAD_DIM)
        mine = lax.all_to_all(parts, ("seq", "chan"), split_axis=0, concat_axis=0, tiled=True)
        gathered.append(mine.reshape(shards, chans, 1, 2, rows, HEAD_DIM))

    outs, sent = (), ()
    for chunk, mine in enumerate(gathered):
        mine, outs, sent = lax.optimization_barrier((mine, outs, sent))
        if chunk > 0:
            outs = unpack(place, *sent, heads * HEAD_DIM, chunk - 1, outs)
        *mixed, keep, send = attention(count, place, start, mine, exchange(mine, 1))
        mixed = [mixed[0]] + [exchange(mixed[d], 2 * d) for d in range(1, group)]
        grads = add(place, keep, exchange(send, 1))
        grads = [grads[0]] + [exchange(grads[d], 2 * d) for d in range(1, group)]
        sent = (mixed, grads)
    return tuple(unpack(place, *sent, heads * HEAD_DIM, len(gathered) - 1, outs))


def solution(mesh):
    spread = P(("seq", "chan"), None)
    in_specs = (P(), spread, spread, spread, spread)
    out_specs = (P("seq", "chan"),) * 4
    return jax.shard_map(
        on_device, mesh=mesh, in_specs=in_specs, out_specs=out_specs, check_vma=False
    )
```

```python
import functools
import math

import jax
import jax.numpy as jnp
from jax import lax
from jax.experimental import pallas as pl
from jax.experimental.pallas import tpu as pltpu
from jax.sharding import PartitionSpec as P

HEAD_DIM = 128
DOC_MAX = 1024
NEG = -1e30
SCALE = HEAD_DIM ** (-0.5)
EXP_SCALE = SCALE * math.log2(math.e)
SCALARS = pl.BlockSpec(memory_space=pltpu.SMEM)
VECTORS = pl.BlockSpec(memory_space=pltpu.VMEM)
ANYWHERE = pl.BlockSpec(memory_space=pl.ANY)


def low_array(*shape):
    return jax.ShapeDtypeStruct(shape, jnp.bfloat16)


def moved(byte_count):
    return pl.CostEstimate(flops=0, bytes_accessed=byte_count, transcendentals=0)


def dot_nt(a, b):
    return lax.dot_general(a, b, (((1,), (1,)), ((), ())), preferred_element_type=jnp.float32)


def dot_nn(a, b):
    return lax.dot_general(a, b, (((1,), (0,)), ((), ())), preferred_element_type=jnp.float32)


def dot_tn(a, b):
    return lax.dot_general(a, b, (((0,), (0,)), ((), ())), preferred_element_type=jnp.float32)


def pack_kernel(group, size, place_ref, *refs):
    query, key, value, cot, out_ref = refs
    core = place_ref[0]
    for chip in range(group):
        for j in range(size):
            columns = slice((chip * size + j) * HEAD_DIM, (chip * size + j + 1) * HEAD_DIM)
            out_ref[2 * chip + core, 0, j, 0] = query[:, columns]
            out_ref[2 * chip + core, 0, j, 1] = cot[:, columns]
            out_ref[2 * chip + 1 - core, 0, j, 0] = key[:, columns]
            out_ref[2 * chip + 1 - core, 0, j, 1] = value[:, columns]


def pack(place, inputs, chans, group, offset, size):
    rows, width = inputs[0].shape
    part = group * size * HEAD_DIM
    per_chan = width // chans // part
    return pl.pallas_call(
        functools.partial(pack_kernel, group, size),
        grid=(chans,),
        out_shape=low_array(2 * group, chans, size, 2, rows, HEAD_DIM),
        in_specs=[SCALARS]
        + [pl.BlockSpec((rows, part), lambda c: (0, c * per_chan + offset // size))] * 4,
        out_specs=pl.BlockSpec(
            (2 * group, 1, size, 2, rows, HEAD_DIM), lambda c: (0, c, 0, 0, 0, 0)
        ),
        cost_estimate=moved(16 * rows * part * chans),
    )(place, *inputs)


def attention_kernel(spans, size, group, *refs):
    count_ref, place_ref, start_ref, mine_ref, other_ref = refs[:5]
    outs, (keep_ref, send_ref) = refs[5 : 5 + group], refs[5 + group : 7 + group]
    pair_ref, key_ref, mixed_ref, key_acc, value_acc, load_sems, sems = refs[7 + group :]
    block = mixed_ref.shape[3]
    core = place_ref[0]
    loads = []
    for j in range(size):
        for m in range(group):
            same, cross = 2 * m + core, 2 * m + 1 - core
            sem = load_sems.at[j, m]
            for k, (source, target) in enumerate(
                (
                    (mine_ref.at[same, :, j], pair_ref.at[j, m]),
                    (mine_ref.at[cross, :, j], key_ref.at[j, cross]),
                    (other_ref.at[same, :, j], key_ref.at[j, same]),
                )
            ):
                loads.append(pltpu.make_async_copy(source, target, sem.at[k]))
    for load in loads:
        load.start()
    key_acc[...] = jnp.zeros_like(key_acc)
    value_acc[...] = jnp.zeros_like(value_acc)
    for load in loads:
        load.wait()

    def work(j, m, span):
        i = 2 * m + core
        low = i - (span - 1)
        width = span * block
        query = pair_ref[j, m, :, 0].reshape(block, HEAD_DIM)
        cot = pair_ref[j, m, :, 1].reshape(block, HEAD_DIM)
        key = key_ref[j, pl.ds(low, span), :, 0].reshape(width, HEAD_DIM)
        value = key_ref[j, pl.ds(low, span), :, 1].reshape(width, HEAD_DIM)
        start = start_ref[pl.ds(pl.multiple_of(i * block, block), block), :] - low * block
        col = lax.broadcasted_iota(jnp.int32, (block, width), 1)
        row = lax.broadcasted_iota(jnp.int32, (block, width), 0) + (span - 1) * block
        allowed = (col >= start) & (col <= row)
        score = jnp.where(allowed, dot_nt(query, key), NEG)
        peak = jnp.max(score, axis=1, keepdims=True)
        expo = jnp.exp2((score - peak) * EXP_SCALE)
        inverse = 1.0 / jnp.sum(expo, axis=1, keepdims=True)
        weight = expo * inverse
        weight_low = weight.astype(jnp.bfloat16)
        mixed = dot_nn(weight_low, value)
        rowdot = jnp.sum(mixed * cot.astype(jnp.float32), axis=1, keepdims=True)
        dscore = (weight * (dot_nt(cot, value) - rowdot)).astype(jnp.bfloat16)
        mixed_ref[m, j, 0] = mixed.astype(jnp.bfloat16)
        mixed_ref[m, j, 1] = (SCALE * dot_nn(dscore, key)).astype(jnp.bfloat16)
        held = pl.ds(pl.multiple_of(low * block, block), width)
        key_acc[j, held, :] += dot_tn(dscore, query)
        value_acc[j, held, :] += dot_tn(weight_low, cot)

    def step(n, carry):
        j, m = n // group, n % group
        for span in range(1, spans + 1):
            pl.when(count_ref[2 * m + core] == span)(functools.partial(work, j, m, span))
        return carry

    lax.fori_loop(0, size * group, step, 0)
    moves = [
        pltpu.make_async_copy(mixed_ref.at[place_ref[1 + d]], outs[d], sems.at[d])
        for d in range(group)
    ]
    for move in moves:
        move.start()

    def finish(n, carry):
        j, m = n // group, n % group
        own = pl.ds(pl.multiple_of((2 * m + core) * block, block), block)
        cross = pl.ds(pl.multiple_of((2 * m + 1 - core) * block, block), block)
        keep_ref[m, j, 0] = SCALE * key_acc[j, own, :]
        keep_ref[m, j, 1] = value_acc[j, own, :]
        send_ref[m, j, 0] = (SCALE * key_acc[j, cross, :]).astype(jnp.bfloat16)
        send_ref[m, j, 1] = value_acc[j, cross, :].astype(jnp.bfloat16)
        return carry

    lax.fori_loop(0, size * group, finish, 0)
    for move in moves:
        move.wait()


def attention(count, place, start, mine, other):
    shards, chans, size, _, rows, _ = mine.shape
    group = shards // 2
    block = chans * rows
    total = shards * block
    spans = min(shards, (DOC_MAX + block - 2) // block + 1)
    pairs = size * group * block * block * min(spans, 3)
    return pl.pallas_call(
        functools.partial(attention_kernel, spans, size, group),
        out_shape=[low_array(size, 2, block, HEAD_DIM)] * group
        + [
            jax.ShapeDtypeStruct((group, size, 2, block, HEAD_DIM), jnp.float32),
            low_array(group, size, 2, block, HEAD_DIM),
        ],
        in_specs=[SCALARS, SCALARS, VECTORS, ANYWHERE, ANYWHERE],
        out_specs=[ANYWHERE] * group + [VECTORS] * 2,
        scratch_shapes=[
            pltpu.VMEM((size, group, chans, 2, rows, HEAD_DIM), jnp.bfloat16),
            pltpu.VMEM((size, shards, chans, 2, rows, HEAD_DIM), jnp.bfloat16),
            pltpu.VMEM((group, size, 2, block, HEAD_DIM), jnp.bfloat16),
            pltpu.VMEM((size, total, HEAD_DIM), jnp.float32),
            pltpu.VMEM((size, total, HEAD_DIM), jnp.float32),
            pltpu.SemaphoreType.DMA((size, group, 3)),
            pltpu.SemaphoreType.DMA((group,)),
        ],
        compiler_params=pltpu.CompilerParams(vmem_limit_bytes=(14 << 20) + 3584 * size * total),
        cost_estimate=pl.CostEstimate(
            flops=12 * HEAD_DIM * pairs,
            bytes_accessed=10 * size * total * HEAD_DIM,
            transcendentals=pairs,
        ),
    )(count, place, start, mine, other)


def add_kernel(place_ref, keep_ref, other_ref, *outs):
    for d, out_ref in enumerate(outs):
        m = place_ref[1 + d]
        out_ref[...] = (keep_ref[m] + other_ref[m].astype(jnp.float32)).astype(jnp.bfloat16)


def add(place, keep, other):
    group = keep.shape[0]
    return pl.pallas_call(
        add_kernel,
        out_shape=[low_array(*keep.shape[1:])] * group,
        in_specs=[SCALARS, VECTORS, VECTORS],
        out_specs=[VECTORS] * group,
        compiler_params=pltpu.CompilerParams(vmem_limit_bytes=32 * 1024 * 1024),
        cost_estimate=moved(8 * keep.size),
    )(place, keep, other)


def unpack_kernel(group, size, offset, place_ref, *refs):
    mixed, grads, outs, sems = refs[:group], refs[group : 2 * group], refs[-5:-1], refs[-1]
    moves = []
    for d in range(group):
        for j in range(size):
            head = (offset * group + place_ref[1 + d]) * size + j
            columns = pl.ds(pl.multiple_of(head * HEAD_DIM, HEAD_DIM), HEAD_DIM)
            for which in range(4):
                source = (mixed if which < 2 else grads)[d].at[j, which % 2]
                moves.append(
                    pltpu.make_async_copy(
                        source, outs[which].at[:, columns], sems.at[d, j, which]
                    )
                )
    for move in moves:
        move.start()
    for move in moves:
        move.wait()


def unpack(place, mixed, grads, width, offset, held):
    group = len(mixed)
    size, _, rows, _ = mixed[0].shape
    return pl.pallas_call(
        functools.partial(unpack_kernel, group, size, offset),
        out_shape=[low_array(rows, width)] * 4,
        in_specs=[SCALARS] + [VECTORS] * (2 * group) + [ANYWHERE] * len(held),
        out_specs=[ANYWHERE] * 4,
        scratch_shapes=[pltpu.SemaphoreType.DMA((group, size, 4))],
        input_output_aliases={1 + 2 * group + i: i for i in range(len(held))},
        compiler_params=pltpu.CompilerParams(vmem_limit_bytes=24 << 20),
        cost_estimate=moved(16 * group * size * rows * HEAD_DIM),
    )(place, *mixed, *grads, *held)


def exchange(value, d):
    return lax.ppermute(value, "seq", [(s, s ^ d) for s in range(lax.axis_size("seq"))])


def on_device(doc_ids, *inputs):
    shards = lax.axis_size("seq")
    chans = lax.axis_size("chan")
    rows, width = inputs[0].shape
    heads = width // HEAD_DIM // chans
    group = shards // 2
    block = rows * chans
    start = jnp.sum((doc_ids[None, :] < doc_ids[:, None]).astype(jnp.int32), axis=1)
    count = jnp.arange(shards, dtype=jnp.int32) - start[::block] // block + 1
    start = start[:, None]
    shard = lax.axis_index("seq")
    chips = jnp.bitwise_xor(shard // 2, jnp.arange(group, dtype=jnp.int32))
    place = jnp.concatenate([(shard % 2)[None].astype(jnp.int32), chips])

    chunks = heads // group
    parts = [
        pack(place, inputs, chans, group, chunk, 1).reshape(shards * chans, 1, 2, rows, HEAD_DIM)
        for chunk in range(chunks)
    ]

    def gather(part):
        part = lax.all_to_all(part, ("seq", "chan"), split_axis=0, concat_axis=0, tiled=True)
        return part.reshape(shards, chans, 1, 2, rows, HEAD_DIM)

    mine = gather(parts[0])
    outs, sent = (), ()
    for chunk in range(chunks):
        later = parts[chunk + 1 :]
        mine, later, outs, sent = lax.optimization_barrier((mine, later, outs, sent))
        following = gather(later[0]) if later else None
        parts[chunk + 1 :] = later
        if chunk > 0:
            outs = unpack(place, *sent, heads * HEAD_DIM, chunk - 1, outs)
        *mixed, keep, send = attention(count, place, start, mine, exchange(mine, 1))
        mixed = [mixed[0]] + [exchange(mixed[d], 2 * d) for d in range(1, group)]
        grads = add(place, keep, exchange(send, 1))
        grads = [grads[0]] + [exchange(grads[d], 2 * d) for d in range(1, group)]
        sent = (mixed, grads)
        mine = following
    return tuple(unpack(place, *sent, heads * HEAD_DIM, chunks - 1, outs))


def solution(mesh):
    spread = P(("seq", "chan"), None)
    in_specs = (P(), spread, spread, spread, spread)
    out_specs = (P("seq", "chan"),) * 4
    return jax.shard_map(
        on_device, mesh=mesh, in_specs=in_specs, out_specs=out_specs, check_vma=False
    )
```

```python
import functools
import math

import jax
import jax.numpy as jnp
from jax import lax
from jax.experimental import pallas as pl
from jax.experimental.pallas import tpu as pltpu
from jax.sharding import PartitionSpec as P

HEAD_DIM = 128
DOC_MAX = 1024
NEG = -1e30
SCALE = HEAD_DIM ** (-0.5)
EXP_SCALE = SCALE * math.log2(math.e)
SCALARS = pl.BlockSpec(memory_space=pltpu.SMEM)
VECTORS = pl.BlockSpec(memory_space=pltpu.VMEM)
ANYWHERE = pl.BlockSpec(memory_space=pl.ANY)


def low_array(*shape):
    return jax.ShapeDtypeStruct(shape, jnp.bfloat16)


def moved(byte_count):
    return pl.CostEstimate(flops=0, bytes_accessed=byte_count, transcendentals=0)


def dot_nt(a, b):
    return lax.dot_general(a, b, (((1,), (1,)), ((), ())), preferred_element_type=jnp.float32)


def dot_nn(a, b):
    return lax.dot_general(a, b, (((1,), (0,)), ((), ())), preferred_element_type=jnp.float32)


def dot_tn(a, b):
    return lax.dot_general(a, b, (((0,), (0,)), ((), ())), preferred_element_type=jnp.float32)


def pack_kernel(group, size, place_ref, *refs):
    query, key, value, cot, out_ref = refs
    core = place_ref[0]
    for chip in range(group):
        for j in range(size):
            columns = slice((chip * size + j) * HEAD_DIM, (chip * size + j + 1) * HEAD_DIM)
            out_ref[2 * chip + core, 0, j, 0] = query[:, columns]
            out_ref[2 * chip + core, 0, j, 1] = cot[:, columns]
            out_ref[2 * chip + 1 - core, 0, j, 0] = key[:, columns]
            out_ref[2 * chip + 1 - core, 0, j, 1] = value[:, columns]


def pack(place, inputs, chans, group, offset, size):
    rows, width = inputs[0].shape
    part = group * size * HEAD_DIM
    per_chan = width // chans // part
    return pl.pallas_call(
        functools.partial(pack_kernel, group, size),
        grid=(chans,),
        out_shape=low_array(2 * group, chans, size, 2, rows, HEAD_DIM),
        in_specs=[SCALARS]
        + [pl.BlockSpec((rows, part), lambda c: (0, c * per_chan + offset // size))] * 4,
        out_specs=pl.BlockSpec(
            (2 * group, 1, size, 2, rows, HEAD_DIM), lambda c: (0, c, 0, 0, 0, 0)
        ),
        cost_estimate=moved(16 * rows * part * chans),
    )(place, *inputs)


def attention_kernel(spans, size, group, *refs):
    count_ref, place_ref, start_ref, mine_ref, other_ref = refs[:5]
    mixed_ref, keep_ref, send_ref, pair_ref, key_ref, key_acc, value_acc, load_sems = refs[5:]
    block = mixed_ref.shape[3]
    core = place_ref[0]
    loads = []
    for j in range(size):
        for m in range(group):
            same, cross = 2 * m + core, 2 * m + 1 - core
            sem = load_sems.at[j, m]
            for k, (source, target) in enumerate(
                (
                    (mine_ref.at[same, :, j], pair_ref.at[j, m]),
                    (mine_ref.at[cross, :, j], key_ref.at[j, cross]),
                    (other_ref.at[same, :, j], key_ref.at[j, same]),
                )
            ):
                loads.append(pltpu.make_async_copy(source, target, sem.at[k]))
    for load in loads:
        load.start()
    key_acc[...] = jnp.zeros_like(key_acc)
    value_acc[...] = jnp.zeros_like(value_acc)
    for load in loads:
        load.wait()

    def work(j, m, span):
        i = 2 * m + core
        low = i - (span - 1)
        width = span * block
        query = pair_ref[j, m, :, 0].reshape(block, HEAD_DIM)
        cot = pair_ref[j, m, :, 1].reshape(block, HEAD_DIM)
        key = key_ref[j, pl.ds(low, span), :, 0].reshape(width, HEAD_DIM)
        value = key_ref[j, pl.ds(low, span), :, 1].reshape(width, HEAD_DIM)
        start = start_ref[pl.ds(pl.multiple_of(i * block, block), block), :] - low * block
        col = lax.broadcasted_iota(jnp.int32, (block, width), 1)
        row = lax.broadcasted_iota(jnp.int32, (block, width), 0) + (span - 1) * block
        allowed = (col >= start) & (col <= row)
        score = jnp.where(allowed, dot_nt(query, key), NEG)
        peak = jnp.max(score, axis=1, keepdims=True)
        expo = jnp.exp2((score - peak) * EXP_SCALE)
        inverse = 1.0 / jnp.sum(expo, axis=1, keepdims=True)
        weight = expo * inverse
        weight_low = weight.astype(jnp.bfloat16)
        mixed = dot_nn(weight_low, value)
        rowdot = jnp.sum(mixed * cot.astype(jnp.float32), axis=1, keepdims=True)
        dscore = (weight * (dot_nt(cot, value) - rowdot)).astype(jnp.bfloat16)
        mixed_ref[m, j, 0] = mixed.astype(jnp.bfloat16)
        mixed_ref[m, j, 1] = (SCALE * dot_nn(dscore, key)).astype(jnp.bfloat16)
        held = pl.ds(pl.multiple_of(low * block, block), width)
        key_acc[j, held, :] += dot_tn(dscore, query)
        value_acc[j, held, :] += dot_tn(weight_low, cot)

    def step(n, carry):
        j, m = n // group, n % group
        for span in range(1, spans + 1):
            pl.when(count_ref[2 * m + core] == span)(functools.partial(work, j, m, span))
        return carry

    lax.fori_loop(0, size * group, step, 0)

    def finish(n, carry):
        j, m = n // group, n % group
        own = pl.ds(pl.multiple_of((2 * m + core) * block, block), block)
        cross = pl.ds(pl.multiple_of((2 * m + 1 - core) * block, block), block)
        keep_ref[m, j, 0] = SCALE * key_acc[j, own, :]
        keep_ref[m, j, 1] = value_acc[j, own, :]
        send_ref[m, j, 0] = (SCALE * key_acc[j, cross, :]).astype(jnp.bfloat16)
        send_ref[m, j, 1] = value_acc[j, cross, :].astype(jnp.bfloat16)
        return carry

    lax.fori_loop(0, size * group, finish, 0)


def attention(count, place, start, mine, other):
    shards, chans, size, _, rows, _ = mine.shape
    group = shards // 2
    block = chans * rows
    total = shards * block
    spans = min(shards, (DOC_MAX + block - 2) // block + 1)
    pairs = size * group * block * block * min(spans, 3)
    return pl.pallas_call(
        functools.partial(attention_kernel, spans, size, group),
        out_shape=[
            low_array(group, size, 2, block, HEAD_DIM),
            jax.ShapeDtypeStruct((group, size, 2, block, HEAD_DIM), jnp.float32),
            low_array(group, size, 2, block, HEAD_DIM),
        ],
        in_specs=[SCALARS, SCALARS, VECTORS, ANYWHERE, ANYWHERE],
        out_specs=[VECTORS] * 3,
        scratch_shapes=[
            pltpu.VMEM((size, group, chans, 2, rows, HEAD_DIM), jnp.bfloat16),
            pltpu.VMEM((size, shards, chans, 2, rows, HEAD_DIM), jnp.bfloat16),
            pltpu.VMEM((size, total, HEAD_DIM), jnp.float32),
            pltpu.VMEM((size, total, HEAD_DIM), jnp.float32),
            pltpu.SemaphoreType.DMA((size, group, 3)),
        ],
        compiler_params=pltpu.CompilerParams(vmem_limit_bytes=(14 << 20) + 3584 * size * total),
        cost_estimate=pl.CostEstimate(
            flops=12 * HEAD_DIM * pairs,
            bytes_accessed=10 * size * total * HEAD_DIM,
            transcendentals=pairs,
        ),
    )(count, place, start, mine, other)


def add_kernel(place_ref, mixed_ref, keep_ref, other_ref, *outs):
    for d, out_ref in enumerate(outs):
        m = place_ref[1 + d]
        total = keep_ref[m] + other_ref[m].astype(jnp.float32)
        out_ref[:, :2] = mixed_ref[m]
        out_ref[:, 2:] = total.astype(jnp.bfloat16)


def add(place, mixed, keep, other):
    group, size, _, block, _ = keep.shape
    return pl.pallas_call(
        add_kernel,
        out_shape=[low_array(size, 4, block, HEAD_DIM)] * group,
        in_specs=[SCALARS] + [VECTORS] * 3,
        out_specs=[VECTORS] * group,
        compiler_params=pltpu.CompilerParams(vmem_limit_bytes=24 << 20),
        cost_estimate=moved(12 * keep.size),
    )(place, mixed, keep, other)


def unpack_kernel(group, size, offset, place_ref, *refs):
    blocks, outs, sems = refs[:group], refs[-5:-1], refs[-1]
    moves = []
    for d in range(group):
        for j in range(size):
            head = (offset * group + place_ref[1 + d]) * size + j
            columns = pl.ds(pl.multiple_of(head * HEAD_DIM, HEAD_DIM), HEAD_DIM)
            for which in range(4):
                moves.append(
                    pltpu.make_async_copy(
                        blocks[d].at[j, which], outs[which].at[:, columns], sems.at[d, j, which]
                    )
                )
    for move in moves:
        move.start()
    for move in moves:
        move.wait()


def unpack(place, blocks, width, offset, held):
    group = len(blocks)
    size, _, rows, _ = blocks[0].shape
    return pl.pallas_call(
        functools.partial(unpack_kernel, group, size, offset),
        out_shape=[low_array(rows, width)] * 4,
        in_specs=[SCALARS] + [VECTORS] * group + [ANYWHERE] * len(held),
        out_specs=[ANYWHERE] * 4,
        scratch_shapes=[pltpu.SemaphoreType.DMA((group, size, 4))],
        input_output_aliases={1 + group + i: i for i in range(len(held))},
        compiler_params=pltpu.CompilerParams(vmem_limit_bytes=24 << 20),
        cost_estimate=moved(16 * group * size * rows * HEAD_DIM),
    )(place, *blocks, *held)


def exchange(value, d):
    return lax.ppermute(value, "seq", [(s, s ^ d) for s in range(lax.axis_size("seq"))])


def on_device(doc_ids, *inputs):
    shards = lax.axis_size("seq")
    chans = lax.axis_size("chan")
    rows, width = inputs[0].shape
    heads = width // HEAD_DIM // chans
    group = shards // 2
    block = rows * chans
    start = jnp.sum((doc_ids[None, :] < doc_ids[:, None]).astype(jnp.int32), axis=1)
    count = jnp.arange(shards, dtype=jnp.int32) - start[::block] // block + 1
    start = start[:, None]
    shard = lax.axis_index("seq")
    chips = jnp.bitwise_xor(shard // 2, jnp.arange(group, dtype=jnp.int32))
    place = jnp.concatenate([(shard % 2)[None].astype(jnp.int32), chips])

    chunks = heads // group
    parts = [
        pack(place, inputs, chans, group, chunk, 1).reshape(shards * chans, 1, 2, rows, HEAD_DIM)
        for chunk in range(chunks)
    ]

    def gather(part):
        part = lax.all_to_all(part, ("seq", "chan"), split_axis=0, concat_axis=0, tiled=True)
        return part.reshape(shards, chans, 1, 2, rows, HEAD_DIM)

    mine = gather(parts[0])
    outs, ready, sent = (), (), ()
    for chunk in range(chunks):
        later = parts[chunk + 1 :]
        mine, later, outs, ready = lax.optimization_barrier((mine, later, outs, ready))
        following = gather(later[0]) if later else None
        parts[chunk + 1 :] = later
        if chunk > 0:
            sent = [ready[0]] + [exchange(ready[d], 2 * d) for d in range(1, group)]
            outs = unpack(place, sent, heads * HEAD_DIM, chunk - 1, outs)
        mixed, keep, send = attention(count, place, start, mine, exchange(mine, 1))
        ready = add(place, mixed, keep, exchange(send, 1))
        mine = following
    sent = [ready[0]] + [exchange(ready[d], 2 * d) for d in range(1, group)]
    return tuple(unpack(place, sent, heads * HEAD_DIM, chunks - 1, outs))


def solution(mesh):
    spread = P(("seq", "chan"), None)
    in_specs = (P(), spread, spread, spread, spread)
    out_specs = (P("seq", "chan"),) * 4
    return jax.shard_map(
        on_device, mesh=mesh, in_specs=in_specs, out_specs=out_specs, check_vma=False
    )
```

```python
import functools
import math

import jax
import jax.numpy as jnp
from jax import lax
from jax.experimental import pallas as pl
from jax.experimental.pallas import tpu as pltpu
from jax.sharding import PartitionSpec as P

HEAD_DIM = 128
DOC_MAX = 1024
NEG = -1e30
SCALE = HEAD_DIM ** (-0.5)
EXP_SCALE = SCALE * math.log2(math.e)
SCALARS = pl.BlockSpec(memory_space=pltpu.SMEM)
VECTORS = pl.BlockSpec(memory_space=pltpu.VMEM)
ANYWHERE = pl.BlockSpec(memory_space=pl.ANY)


def low_array(*shape):
    return jax.ShapeDtypeStruct(shape, jnp.bfloat16)


def moved(byte_count):
    return pl.CostEstimate(flops=0, bytes_accessed=byte_count, transcendentals=0)


def dot_nt(a, b):
    return lax.dot_general(a, b, (((1,), (1,)), ((), ())), preferred_element_type=jnp.float32)


def dot_nn(a, b):
    return lax.dot_general(a, b, (((1,), (0,)), ((), ())), preferred_element_type=jnp.float32)


def dot_tn(a, b):
    return lax.dot_general(a, b, (((0,), (0,)), ((), ())), preferred_element_type=jnp.float32)


def pack_kernel(group, size, place_ref, *refs):
    query, key, value, cot, out_ref = refs
    core = place_ref[0]
    for chip in range(group):
        for j in range(size):
            columns = slice((chip * size + j) * HEAD_DIM, (chip * size + j + 1) * HEAD_DIM)
            out_ref[2 * chip + core, 0, j, 0] = query[:, columns]
            out_ref[2 * chip + core, 0, j, 1] = cot[:, columns]
            out_ref[2 * chip + 1 - core, 0, j, 0] = key[:, columns]
            out_ref[2 * chip + 1 - core, 0, j, 1] = value[:, columns]


def pack(place, inputs, chans, group, offset, size):
    rows, width = inputs[0].shape
    part = group * size * HEAD_DIM
    per_chan = width // chans // part
    return pl.pallas_call(
        functools.partial(pack_kernel, group, size),
        grid=(chans,),
        out_shape=low_array(2 * group, chans, size, 2, rows, HEAD_DIM),
        in_specs=[SCALARS]
        + [pl.BlockSpec((rows, part), lambda c: (0, c * per_chan + offset // size))] * 4,
        out_specs=pl.BlockSpec(
            (2 * group, 1, size, 2, rows, HEAD_DIM), lambda c: (0, c, 0, 0, 0, 0)
        ),
        cost_estimate=moved(16 * rows * part * chans),
    )(place, *inputs)


def attention_kernel(spans, size, group, *refs):
    count_ref, place_ref, start_ref, mine_ref, other_ref = refs[:5]
    mixed_ref, keep_ref, send_ref, pair_ref, key_ref, key_acc, value_acc, load_sems = refs[5:]
    block = mixed_ref.shape[3]
    core = place_ref[0]
    loads = []
    for j in range(size):
        for m in range(group):
            same, cross = 2 * m + core, 2 * m + 1 - core
            sem = load_sems.at[j, m]
            for k, (source, target) in enumerate(
                (
                    (mine_ref.at[same, :, j], pair_ref.at[j, m]),
                    (mine_ref.at[cross, :, j], key_ref.at[j, cross]),
                    (other_ref.at[same, :, j], key_ref.at[j, same]),
                )
            ):
                loads.append(pltpu.make_async_copy(source, target, sem.at[k]))
    for load in loads:
        load.start()
    key_acc[...] = jnp.zeros_like(key_acc)
    value_acc[...] = jnp.zeros_like(value_acc)
    for load in loads:
        load.wait()

    def work(j, m, span):
        i = 2 * m + core
        low = i - (span - 1)
        width = span * block
        query = pair_ref[j, m, :, 0].reshape(block, HEAD_DIM)
        cot = pair_ref[j, m, :, 1].reshape(block, HEAD_DIM)
        key = key_ref[j, pl.ds(low, span), :, 0].reshape(width, HEAD_DIM)
        value = key_ref[j, pl.ds(low, span), :, 1].reshape(width, HEAD_DIM)
        start = start_ref[pl.ds(pl.multiple_of(i * block, block), block), :] - low * block
        col = lax.broadcasted_iota(jnp.int32, (block, width), 1)
        row = lax.broadcasted_iota(jnp.int32, (block, width), 0) + (span - 1) * block
        allowed = (col >= start) & (col <= row)
        score = jnp.where(allowed, dot_nt(query, key), NEG)
        peak = jnp.max(score, axis=1, keepdims=True)
        expo = jnp.exp2((score - peak) * EXP_SCALE)
        inverse = 1.0 / jnp.sum(expo, axis=1, keepdims=True)
        weight = expo * inverse
        weight_low = weight.astype(jnp.bfloat16)
        mixed = dot_nn(weight_low, value)
        rowdot = jnp.sum(mixed * cot.astype(jnp.float32), axis=1, keepdims=True)
        dscore = (weight * (dot_nt(cot, value) - rowdot)).astype(jnp.bfloat16)
        mixed_ref[m, j, 0] = mixed.astype(jnp.bfloat16)
        mixed_ref[m, j, 1] = (SCALE * dot_nn(dscore, key)).astype(jnp.bfloat16)
        held = pl.ds(pl.multiple_of(low * block, block), width)
        key_acc[j, held, :] += dot_tn(dscore, query)
        value_acc[j, held, :] += dot_tn(weight_low, cot)

    def step(n, carry):
        j, m = n // group, n % group
        for span in range(1, spans + 1):
            pl.when(count_ref[2 * m + core] == span)(functools.partial(work, j, m, span))
        return carry

    lax.fori_loop(0, size * group, step, 0)

    def finish(n, carry):
        j, m = n // group, n % group
        own = pl.ds(pl.multiple_of((2 * m + core) * block, block), block)
        cross = pl.ds(pl.multiple_of((2 * m + 1 - core) * block, block), block)
        keep_ref[m, j, 0] = SCALE * key_acc[j, own, :]
        keep_ref[m, j, 1] = value_acc[j, own, :]
        send_ref[m, j, 0] = (SCALE * key_acc[j, cross, :]).astype(jnp.bfloat16)
        send_ref[m, j, 1] = value_acc[j, cross, :].astype(jnp.bfloat16)
        return carry

    lax.fori_loop(0, size * group, finish, 0)


def attention(count, place, start, mine, other):
    shards, chans, size, _, rows, _ = mine.shape
    group = shards // 2
    block = chans * rows
    total = shards * block
    spans = min(shards, (DOC_MAX + block - 2) // block + 1)
    pairs = size * group * block * block * min(spans, 3)
    return pl.pallas_call(
        functools.partial(attention_kernel, spans, size, group),
        out_shape=[
            low_array(group, size, 2, block, HEAD_DIM),
            jax.ShapeDtypeStruct((group, size, 2, block, HEAD_DIM), jnp.float32),
            low_array(group, size, 2, block, HEAD_DIM),
        ],
        in_specs=[SCALARS, SCALARS, VECTORS, ANYWHERE, ANYWHERE],
        out_specs=[VECTORS] * 3,
        scratch_shapes=[
            pltpu.VMEM((size, group, chans, 2, rows, HEAD_DIM), jnp.bfloat16),
            pltpu.VMEM((size, shards, chans, 2, rows, HEAD_DIM), jnp.bfloat16),
            pltpu.VMEM((size, total, HEAD_DIM), jnp.float32),
            pltpu.VMEM((size, total, HEAD_DIM), jnp.float32),
            pltpu.SemaphoreType.DMA((size, group, 3)),
        ],
        compiler_params=pltpu.CompilerParams(vmem_limit_bytes=(14 << 20) + 3584 * size * total),
        cost_estimate=pl.CostEstimate(
            flops=12 * HEAD_DIM * pairs,
            bytes_accessed=10 * size * total * HEAD_DIM,
            transcendentals=pairs,
        ),
    )(count, place, start, mine, other)


def add_kernel(place_ref, mixed_ref, keep_ref, other_ref, *outs):
    for d, out_ref in enumerate(outs):
        m = place_ref[1 + d]
        total = keep_ref[m] + other_ref[m].astype(jnp.float32)
        out_ref[:, :2] = mixed_ref[m]
        out_ref[:, 2:] = total.astype(jnp.bfloat16)


def add(place, mixed, keep, other):
    group, size, _, block, _ = keep.shape
    return pl.pallas_call(
        add_kernel,
        out_shape=[low_array(size, 4, block, HEAD_DIM)] * group,
        in_specs=[SCALARS] + [VECTORS] * 3,
        out_specs=[VECTORS] * group,
        compiler_params=pltpu.CompilerParams(vmem_limit_bytes=24 << 20),
        cost_estimate=moved(12 * keep.size),
    )(place, mixed, keep, other)


def unpack_kernel(group, size, offset, place_ref, *refs):
    blocks, outs, sems = refs[:group], refs[-5:-1], refs[-1]
    moves = []
    for d in range(group):
        for j in range(size):
            head = (offset * group + place_ref[1 + d]) * size + j
            columns = pl.ds(pl.multiple_of(head * HEAD_DIM, HEAD_DIM), HEAD_DIM)
            for which in range(4):
                moves.append(
                    pltpu.make_async_copy(
                        blocks[d].at[j, which], outs[which].at[:, columns], sems.at[d, j, which]
                    )
                )
    for move in moves:
        move.start()
    for move in moves:
        move.wait()


def unpack(place, blocks, width, offset, held):
    group = len(blocks)
    size, _, rows, _ = blocks[0].shape
    return pl.pallas_call(
        functools.partial(unpack_kernel, group, size, offset),
        out_shape=[low_array(rows, width)] * 4,
        in_specs=[SCALARS] + [VECTORS] * group + [ANYWHERE] * len(held),
        out_specs=[ANYWHERE] * 4,
        scratch_shapes=[pltpu.SemaphoreType.DMA((group, size, 4))],
        input_output_aliases={1 + group + i: i for i in range(len(held))},
        compiler_params=pltpu.CompilerParams(vmem_limit_bytes=24 << 20),
        cost_estimate=moved(16 * group * size * rows * HEAD_DIM),
    )(place, *blocks, *held)


def exchange(value, d):
    return lax.ppermute(value, "seq", [(s, s ^ d) for s in range(lax.axis_size("seq"))])


def on_device(doc_ids, *inputs):
    shards = lax.axis_size("seq")
    chans = lax.axis_size("chan")
    rows, width = inputs[0].shape
    heads = width // HEAD_DIM // chans
    group = shards // 2
    block = rows * chans
    start = jnp.sum((doc_ids[None, :] < doc_ids[:, None]).astype(jnp.int32), axis=1)
    count = jnp.arange(shards, dtype=jnp.int32) - start[::block] // block + 1
    start = start[:, None]
    shard = lax.axis_index("seq")
    chips = jnp.bitwise_xor(shard // 2, jnp.arange(group, dtype=jnp.int32))
    place = jnp.concatenate([(shard % 2)[None].astype(jnp.int32), chips])

    chunks = heads // group
    parts = [
        pack(place, inputs, chans, group, chunk, 1).reshape(shards * chans, 1, 2, rows, HEAD_DIM)
        for chunk in range(chunks)
    ]

    def gather(part):
        part = lax.all_to_all(part, ("seq", "chan"), split_axis=0, concat_axis=0, tiled=True)
        return part.reshape(shards, chans, 1, 2, rows, HEAD_DIM)

    mine = gather(parts[0])
    outs, ready, sent = (), (), ()
    for chunk in range(chunks):
        later = parts[chunk + 1 :]
        mine, later, outs, ready = lax.optimization_barrier((mine, later, outs, ready))
        following = gather(later[0]) if later else None
        parts[chunk + 1 :] = later
        if chunk > 0:
            sent = [ready[0]] + [exchange(ready[d], 2 * d) for d in range(1, group)]
        mixed, keep, send = attention(count, place, start, mine, exchange(mine, 1))
        if chunk > 0:
            send, sent = lax.optimization_barrier((send, sent))
            outs = unpack(place, sent, heads * HEAD_DIM, chunk - 1, outs)
        ready = add(place, mixed, keep, exchange(send, 1))
        mine = following
    sent = [ready[0]] + [exchange(ready[d], 2 * d) for d in range(1, group)]
    return tuple(unpack(place, sent, heads * HEAD_DIM, chunks - 1, outs))


def solution(mesh):
    spread = P(("seq", "chan"), None)
    in_specs = (P(), spread, spread, spread, spread)
    out_specs = (P("seq", "chan"),) * 4
    return jax.shard_map(
        on_device, mesh=mesh, in_specs=in_specs, out_specs=out_specs, check_vma=False
    )
```

```python
import functools
import math

import jax
import jax.numpy as jnp
from jax import lax
from jax.experimental import pallas as pl
from jax.experimental.pallas import tpu as pltpu
from jax.sharding import PartitionSpec as P

HEAD_DIM = 128
DOC_MAX = 1024
NEG = -1e30
SCALE = HEAD_DIM ** (-0.5)
EXP_SCALE = SCALE * math.log2(math.e)
SCALARS = pl.BlockSpec(memory_space=pltpu.SMEM)
VECTORS = pl.BlockSpec(memory_space=pltpu.VMEM)
ANYWHERE = pl.BlockSpec(memory_space=pl.ANY)


def low_array(*shape):
    return jax.ShapeDtypeStruct(shape, jnp.bfloat16)


def moved(byte_count):
    return pl.CostEstimate(flops=0, bytes_accessed=byte_count, transcendentals=0)


def dot_nt(a, b):
    return lax.dot_general(a, b, (((1,), (1,)), ((), ())), preferred_element_type=jnp.float32)


def dot_nn(a, b):
    return lax.dot_general(a, b, (((1,), (0,)), ((), ())), preferred_element_type=jnp.float32)


def dot_tn(a, b):
    return lax.dot_general(a, b, (((0,), (0,)), ((), ())), preferred_element_type=jnp.float32)


def pack_kernel(group, size, place_ref, *refs):
    query, key, value, cot, out_ref = refs
    core = place_ref[0]
    for chip in range(group):
        for j in range(size):
            columns = slice((chip * size + j) * HEAD_DIM, (chip * size + j + 1) * HEAD_DIM)
            out_ref[2 * chip + core, 0, j, 0] = query[:, columns]
            out_ref[2 * chip + core, 0, j, 1] = cot[:, columns]
            out_ref[2 * chip + 1 - core, 0, j, 0] = key[:, columns]
            out_ref[2 * chip + 1 - core, 0, j, 1] = value[:, columns]


def pack(place, inputs, chans, group, offset, size):
    rows, width = inputs[0].shape
    part = group * size * HEAD_DIM
    per_chan = width // chans // part
    return pl.pallas_call(
        functools.partial(pack_kernel, group, size),
        grid=(chans,),
        out_shape=low_array(2 * group, chans, size, 2, rows, HEAD_DIM),
        in_specs=[SCALARS]
        + [pl.BlockSpec((rows, part), lambda c: (0, c * per_chan + offset // size))] * 4,
        out_specs=pl.BlockSpec(
            (2 * group, 1, size, 2, rows, HEAD_DIM), lambda c: (0, c, 0, 0, 0, 0)
        ),
        cost_estimate=moved(16 * rows * part * chans),
    )(place, *inputs)


def attention_kernel(spans, size, group, *refs):
    count_ref, place_ref, start_ref, mine_ref, other_ref = refs[:5]
    mixed_ref, keep_ref, send_ref, pair_ref, key_ref, key_acc, value_acc, load_sems = refs[5:]
    block = mixed_ref.shape[3]
    core = place_ref[0]
    loads = []
    for j in range(size):
        for m in range(group):
            same, cross = 2 * m + core, 2 * m + 1 - core
            sem = load_sems.at[j, m]
            for k, (source, target) in enumerate(
                (
                    (mine_ref.at[same, :, j], pair_ref.at[j, m]),
                    (mine_ref.at[cross, :, j], key_ref.at[j, cross]),
                    (other_ref.at[same, :, j], key_ref.at[j, same]),
                )
            ):
                loads.append(pltpu.make_async_copy(source, target, sem.at[k]))
    for load in loads:
        load.start()
    key_acc[...] = jnp.zeros_like(key_acc)
    value_acc[...] = jnp.zeros_like(value_acc)
    for load in loads:
        load.wait()

    def work(j, m, span):
        i = 2 * m + core
        low = i - (span - 1)
        width = span * block
        query = pair_ref[j, m, :, 0].reshape(block, HEAD_DIM)
        cot = pair_ref[j, m, :, 1].reshape(block, HEAD_DIM)
        key = key_ref[j, pl.ds(low, span), :, 0].reshape(width, HEAD_DIM)
        value = key_ref[j, pl.ds(low, span), :, 1].reshape(width, HEAD_DIM)
        start = start_ref[pl.ds(pl.multiple_of(i * block, block), block), :] - low * block
        col = lax.broadcasted_iota(jnp.int32, (block, width), 1)
        row = lax.broadcasted_iota(jnp.int32, (block, width), 0) + (span - 1) * block
        allowed = (col >= start) & (col <= row)
        score = jnp.where(allowed, dot_nt(query, key), NEG)
        peak = jnp.max(score, axis=1, keepdims=True)
        expo = jnp.exp2((score - peak) * EXP_SCALE)
        inverse = 1.0 / jnp.sum(expo, axis=1, keepdims=True)
        weight = expo * inverse
        weight_low = weight.astype(jnp.bfloat16)
        mixed = dot_nn(weight_low, value)
        rowdot = jnp.sum(mixed * cot.astype(jnp.float32), axis=1, keepdims=True)
        dscore = (weight * (dot_nt(cot, value) - rowdot)).astype(jnp.bfloat16)
        mixed_ref[m, j, 0] = mixed.astype(jnp.bfloat16)
        mixed_ref[m, j, 1] = (SCALE * dot_nn(dscore, key)).astype(jnp.bfloat16)
        held = pl.ds(pl.multiple_of(low * block, block), width)
        key_acc[j, held, :] += dot_tn(dscore, query)
        value_acc[j, held, :] += dot_tn(weight_low, cot)

    def step(n, carry):
        j, m = n // group, n % group
        for span in range(1, spans + 1):
            pl.when(count_ref[2 * m + core] == span)(functools.partial(work, j, m, span))
        return carry

    lax.fori_loop(0, size * group, step, 0)

    def finish(n, carry):
        j, m = n // group, n % group
        own = pl.ds(pl.multiple_of((2 * m + core) * block, block), block)
        cross = pl.ds(pl.multiple_of((2 * m + 1 - core) * block, block), block)
        keep_ref[m, j, 0] = SCALE * key_acc[j, own, :]
        keep_ref[m, j, 1] = value_acc[j, own, :]
        send_ref[m, j, 0] = (SCALE * key_acc[j, cross, :]).astype(jnp.bfloat16)
        send_ref[m, j, 1] = value_acc[j, cross, :].astype(jnp.bfloat16)
        return carry

    lax.fori_loop(0, size * group, finish, 0)


def attention(count, place, start, mine, other):
    shards, chans, size, _, rows, _ = mine.shape
    group = shards // 2
    block = chans * rows
    total = shards * block
    spans = min(shards, (DOC_MAX + block - 2) // block + 1)
    pairs = size * group * block * block * min(spans, 3)
    return pl.pallas_call(
        functools.partial(attention_kernel, spans, size, group),
        out_shape=[
            low_array(group, size, 2, block, HEAD_DIM),
            jax.ShapeDtypeStruct((group, size, 2, block, HEAD_DIM), jnp.float32),
            low_array(group, size, 2, block, HEAD_DIM),
        ],
        in_specs=[SCALARS, SCALARS, VECTORS, ANYWHERE, ANYWHERE],
        out_specs=[VECTORS] * 3,
        scratch_shapes=[
            pltpu.VMEM((size, group, chans, 2, rows, HEAD_DIM), jnp.bfloat16),
            pltpu.VMEM((size, shards, chans, 2, rows, HEAD_DIM), jnp.bfloat16),
            pltpu.VMEM((size, total, HEAD_DIM), jnp.float32),
            pltpu.VMEM((size, total, HEAD_DIM), jnp.float32),
            pltpu.SemaphoreType.DMA((size, group, 3)),
        ],
        compiler_params=pltpu.CompilerParams(vmem_limit_bytes=(14 << 20) + 3584 * size * total),
        cost_estimate=pl.CostEstimate(
            flops=12 * HEAD_DIM * pairs,
            bytes_accessed=10 * size * total * HEAD_DIM,
            transcendentals=pairs,
        ),
    )(count, place, start, mine, other)


def add_kernel(place_ref, mixed_ref, keep_ref, other_ref, *outs):
    for d, out_ref in enumerate(outs):
        m = place_ref[1 + d]
        total = keep_ref[m] + other_ref[m].astype(jnp.float32)
        out_ref[:, :2] = mixed_ref[m]
        out_ref[:, 2:] = total.astype(jnp.bfloat16)


def add(place, mixed, keep, other):
    group, size, _, block, _ = keep.shape
    return pl.pallas_call(
        add_kernel,
        out_shape=[low_array(size, 4, block, HEAD_DIM)] * group,
        in_specs=[SCALARS] + [VECTORS] * 3,
        out_specs=[VECTORS] * group,
        compiler_params=pltpu.CompilerParams(vmem_limit_bytes=24 << 20),
        cost_estimate=moved(12 * keep.size),
    )(place, mixed, keep, other)


def unpack_kernel(group, size, offset, place_ref, *refs):
    blocks, outs, sems = refs[:group], refs[-5:-1], refs[-1]
    moves = []
    for d in range(group):
        for j in range(size):
            head = (offset * group + place_ref[1 + d]) * size + j
            columns = pl.ds(pl.multiple_of(head * HEAD_DIM, HEAD_DIM), HEAD_DIM)
            for which in range(4):
                moves.append(
                    pltpu.make_async_copy(
                        blocks[d].at[j, which], outs[which].at[:, columns], sems.at[d, j, which]
                    )
                )
    for move in moves:
        move.start()
    for move in moves:
        move.wait()


def unpack(place, blocks, width, offset, held):
    group = len(blocks)
    size, _, rows, _ = blocks[0].shape
    return pl.pallas_call(
        functools.partial(unpack_kernel, group, size, offset),
        out_shape=[low_array(rows, width)] * 4,
        in_specs=[SCALARS] + [VECTORS] * group + [ANYWHERE] * len(held),
        out_specs=[ANYWHERE] * 4,
        scratch_shapes=[pltpu.SemaphoreType.DMA((group, size, 4))],
        input_output_aliases={1 + group + i: i for i in range(len(held))},
        compiler_params=pltpu.CompilerParams(vmem_limit_bytes=24 << 20),
        cost_estimate=moved(16 * group * size * rows * HEAD_DIM),
    )(place, *blocks, *held)


def exchange(value, d):
    return lax.ppermute(value, "seq", [(s, s ^ d) for s in range(lax.axis_size("seq"))])


def on_device(doc_ids, *inputs):
    shards = lax.axis_size("seq")
    chans = lax.axis_size("chan")
    rows, width = inputs[0].shape
    heads = width // HEAD_DIM // chans
    group = shards // 2
    block = rows * chans
    start = jnp.sum((doc_ids[None, :] < doc_ids[:, None]).astype(jnp.int32), axis=1)
    count = jnp.arange(shards, dtype=jnp.int32) - start[::block] // block + 1
    start = start[:, None]
    shard = lax.axis_index("seq")
    chips = jnp.bitwise_xor(shard // 2, jnp.arange(group, dtype=jnp.int32))
    place = jnp.concatenate([(shard % 2)[None].astype(jnp.int32), chips])

    chunks = heads // group
    parts = [
        pack(place, inputs, chans, group, chunk, 1).reshape(shards * chans, 1, 2, rows, HEAD_DIM)
        for chunk in range(chunks)
    ]

    def gather(part):
        part = lax.all_to_all(part, ("seq", "chan"), split_axis=0, concat_axis=0, tiled=True)
        return part.reshape(shards, chans, 1, 2, rows, HEAD_DIM)

    def spread(ready):
        return [ready[0]] + [exchange(ready[d], 2 * d) for d in range(1, group)]

    tied = lax.optimization_barrier
    mine, parts = tied((gather(parts[0]), parts[1:]))
    outs, sent, partial = (), (), None
    for chunk in range(chunks):
        following = None
        if partial:
            parts, partial = tied((parts, partial))
        if parts:
            following, parts = gather(parts[0]), parts[1:]
        if partial:
            mine, partial = tied((mine, partial))
            if sent:
                partial, sent = tied((partial, sent))
                outs = unpack(place, sent, heads * HEAD_DIM, chunk - 2, outs)
            mixed, keep, send = partial
            ready = add(place, mixed, keep, exchange(send, 1))
            mine, ready, outs = tied((mine, ready, outs))
            sent = spread(ready)
        partial = attention(count, place, start, mine, exchange(mine, 1))
        mine = following
    if sent:
        partial, sent = tied((partial, sent))
        outs = unpack(place, sent, heads * HEAD_DIM, chunks - 2, outs)
    mixed, keep, send = partial
    ready = add(place, mixed, keep, exchange(send, 1))
    return tuple(unpack(place, spread(ready), heads * HEAD_DIM, chunks - 1, outs))


def solution(mesh):
    spread = P(("seq", "chan"), None)
    in_specs = (P(), spread, spread, spread, spread)
    out_specs = (P("seq", "chan"),) * 4
    return jax.shard_map(
        on_device, mesh=mesh, in_specs=in_specs, out_specs=out_specs, check_vma=False
    )
```

```python
import functools
import math

import jax
import jax.numpy as jnp
from jax import lax
from jax.experimental import pallas as pl
from jax.experimental.pallas import tpu as pltpu
from jax.sharding import PartitionSpec as P

HEAD_DIM = 128
DOC_MAX = 1024
NEG = -1e30
SCALE = HEAD_DIM ** (-0.5)
EXP_SCALE = SCALE * math.log2(math.e)
SCALARS = pl.BlockSpec(memory_space=pltpu.SMEM)
VECTORS = pl.BlockSpec(memory_space=pltpu.VMEM)
ANYWHERE = pl.BlockSpec(memory_space=pl.ANY)


def low_array(*shape):
    return jax.ShapeDtypeStruct(shape, jnp.bfloat16)


def moved(byte_count):
    return pl.CostEstimate(flops=0, bytes_accessed=byte_count, transcendentals=0)


def dot_nt(a, b):
    return lax.dot_general(a, b, (((1,), (1,)), ((), ())), preferred_element_type=jnp.float32)


def dot_nn(a, b):
    return lax.dot_general(a, b, (((1,), (0,)), ((), ())), preferred_element_type=jnp.float32)


def dot_tn(a, b):
    return lax.dot_general(a, b, (((0,), (0,)), ((), ())), preferred_element_type=jnp.float32)


def pack_kernel(owners, *refs):
    ins, out_ref = refs[:4], refs[4]
    for owner in range(owners):
        for which in range(4):
            out_ref[owner, 0, which] = ins[which][:, owner * HEAD_DIM : (owner + 1) * HEAD_DIM]


def pack(inputs, chans, turns, turn):
    rows, width = inputs[0].shape
    owners = width // HEAD_DIM // chans // turns
    return pl.pallas_call(
        functools.partial(pack_kernel, owners),
        grid=(chans,),
        out_shape=low_array(owners, chans, 4, rows, HEAD_DIM),
        in_specs=[pl.BlockSpec((rows, owners * HEAD_DIM), lambda c: (0, c * turns + turn))] * 4,
        out_specs=pl.BlockSpec((owners, 1, 4, rows, HEAD_DIM), lambda c: (0, c, 0, 0, 0)),
        cost_estimate=moved(16 * rows * width // turns),
    )(*inputs)


def attention_kernel(spans, count_ref, start_ref, target_ref, in_ref, *refs):
    outs, (mixed_ref, key_acc, value_acc) = refs[:-3], refs[-3:]
    blocks, _, block, _ = mixed_ref.shape
    key_acc[...] = jnp.zeros_like(key_acc)
    value_acc[...] = jnp.zeros_like(value_acc)

    def tokens(which, first, count):
        return in_ref[pl.ds(first, count), :, which].reshape(count * block, HEAD_DIM)

    def work(i, span):
        low = i - (span - 1)
        width = span * block
        query = tokens(0, i, 1)
        cot = tokens(3, i, 1).astype(jnp.float32)
        key = tokens(1, low, span)
        value = tokens(2, low, span)
        start = start_ref[pl.ds(pl.multiple_of(i * block, block), block), :] - low * block
        col = lax.broadcasted_iota(jnp.int32, (block, width), 1)
        row = lax.broadcasted_iota(jnp.int32, (block, width), 0) + (span - 1) * block
        allowed = (col >= start) & (col <= row)
        score = jnp.where(allowed, dot_nt(query, key), NEG)
        peak = jnp.max(score, axis=1, keepdims=True)
        expo = jnp.exp2((score - peak) * EXP_SCALE)
        inverse = 1.0 / jnp.sum(expo, axis=1, keepdims=True)
        expo_low = expo.astype(jnp.bfloat16)
        mixed = dot_nn(expo_low, value) * inverse
        scaled = cot * inverse
        scaled_low = scaled.astype(jnp.bfloat16)
        rowdot = jnp.sum(mixed * scaled, axis=1, keepdims=True)
        dscore = (expo * (dot_nt(scaled_low, value) - rowdot)).astype(jnp.bfloat16)
        mixed_ref[i, 0] = mixed.astype(jnp.bfloat16)
        mixed_ref[i, 1] = (SCALE * dot_nn(dscore, key)).astype(jnp.bfloat16)
        held = pl.ds(pl.multiple_of(low * block, block), width)
        key_acc[held, :] += dot_tn(dscore, query)
        value_acc[held, :] += dot_tn(expo_low, scaled_low)

    def step(i, carry):
        for span in range(1, spans + 1):
            pl.when(count_ref[i] == span)(functools.partial(work, i, span))
        return carry

    lax.fori_loop(0, blocks, step, 0)
    for d, out_ref in enumerate(outs):
        i = target_ref[d]
        held = pl.ds(pl.multiple_of(i * block, block), block)
        out_ref[:2] = mixed_ref[i]
        out_ref[2] = (SCALE * key_acc[held, :]).astype(jnp.bfloat16)
        out_ref[3] = value_acc[held, :].astype(jnp.bfloat16)


def attention(count, start, targets, packed):
    shards, chans, _, rows, _ = packed.shape
    block = chans * rows
    total = shards * block
    spans = min(shards, (DOC_MAX + block - 2) // block + 1)
    pairs = total * block * min(spans, 3)
    return pl.pallas_call(
        functools.partial(attention_kernel, spans),
        out_shape=[low_array(4, block, HEAD_DIM)] * shards,
        in_specs=[SCALARS, VECTORS, SCALARS, VECTORS],
        out_specs=[VECTORS] * shards,
        scratch_shapes=[
            pltpu.VMEM((shards, 2, block, HEAD_DIM), jnp.bfloat16),
            pltpu.VMEM((total, HEAD_DIM), jnp.float32),
            pltpu.VMEM((total, HEAD_DIM), jnp.float32),
        ],
        compiler_params=pltpu.CompilerParams(vmem_limit_bytes=(16 << 20) + 3840 * total),
        cost_estimate=pl.CostEstimate(
            flops=12 * HEAD_DIM * pairs, bytes_accessed=16 * total * HEAD_DIM, transcendentals=pairs
        ),
    )(count, start, targets, packed)


def unpack_kernel(count, column_ref, *refs):
    blocks, outs, sems = refs[:count], refs[-5:-1], refs[-1]
    moves = []
    for b in range(count):
        columns = pl.ds(pl.multiple_of(column_ref[b] * HEAD_DIM, HEAD_DIM), HEAD_DIM)
        for which in range(4):
            moves.append(
                pltpu.make_async_copy(
                    blocks[b].at[which], outs[which].at[:, columns], sems.at[b, which]
                )
            )
    for move in moves:
        move.start()
    for move in moves:
        move.wait()


def unpack(blocks, columns, width, held):
    count = len(blocks)
    rows = blocks[0].shape[1]
    return pl.pallas_call(
        functools.partial(unpack_kernel, count),
        out_shape=[low_array(rows, width)] * 4,
        in_specs=[SCALARS] + [VECTORS] * count + [ANYWHERE] * len(held),
        out_specs=[ANYWHERE] * 4,
        scratch_shapes=[pltpu.SemaphoreType.DMA((count, 4))],
        input_output_aliases={1 + count + i: i for i in range(len(held))},
        compiler_params=pltpu.CompilerParams(vmem_limit_bytes=16 << 20),
        cost_estimate=moved(16 * count * rows * HEAD_DIM),
    )(columns, *blocks, *held)


def exchange(value, d):
    return lax.ppermute(value, "seq", [(s, s ^ d) for s in range(lax.axis_size("seq"))])


def on_device(doc_ids, *inputs):
    shards = lax.axis_size("seq")
    chans = lax.axis_size("chan")
    rows, width = inputs[0].shape
    heads = width // HEAD_DIM // chans
    turns = max(1, heads // shards)
    owners = heads // turns
    copies = shards // owners
    block = rows * chans
    start = jnp.sum((doc_ids[None, :] < doc_ids[:, None]).astype(jnp.int32), axis=1)
    count = jnp.arange(shards, dtype=jnp.int32) - start[::block] // block + 1
    start = start[:, None]
    peers = jnp.bitwise_xor(lax.axis_index("seq"), jnp.arange(shards, dtype=jnp.int32))
    tied = lax.optimization_barrier

    def gather(parts):
        parts = jnp.repeat(parts, copies, axis=0) if copies > 1 else parts
        parts = parts.reshape(shards * chans, 4, rows, HEAD_DIM)
        parts = lax.all_to_all(parts, ("seq", "chan"), split_axis=0, concat_axis=0, tiled=True)
        return parts.reshape(shards, chans, 4, rows, HEAD_DIM)

    parts = [pack(inputs, chans, turns, turn) for turn in range(turns)]
    mine, parts = tied((gather(parts[0]), parts[1:]))
    outs, blocks = (), ()
    for turn in range(turns):
        following = gather(parts[turn]) if turn + 1 < turns else None
        mine, blocks = tied((mine, blocks))
        if turn > 0:
            outs = unpack(blocks, columns, heads * HEAD_DIM, outs)
        blocks = list(attention(count, start, peers, mine))
        if copies == 1:
            blocks = [blocks[0]] + [exchange(blocks[d], d) for d in range(1, shards)]
            columns = peers + turn * owners
        else:
            order = jnp.stack(blocks)[peers]
            order = lax.all_to_all(order, "seq", split_axis=0, concat_axis=0, tiled=True)
            blocks = [order[owner * copies] for owner in range(owners)]
            columns = jnp.arange(owners, dtype=jnp.int32)
        mine = following
    return tuple(unpack(blocks, columns, heads * HEAD_DIM, outs))


def solution(mesh):
    spread = P(("seq", "chan"), None)
    in_specs = (P(), spread, spread, spread, spread)
    out_specs = (P("seq", "chan"),) * 4
    return jax.shard_map(
        on_device, mesh=mesh, in_specs=in_specs, out_specs=out_specs, check_vma=False
    )
```

```python
import functools
import math

import jax
import jax.numpy as jnp
from jax import lax
from jax.experimental import pallas as pl
from jax.experimental.pallas import tpu as pltpu
from jax.sharding import PartitionSpec as P

HEAD_DIM = 128
DOC_MAX = 1024
NEG = -1e30
SCALE = HEAD_DIM ** (-0.5)
EXP_SCALE = SCALE * math.log2(math.e)
SCALARS = pl.BlockSpec(memory_space=pltpu.SMEM)
VECTORS = pl.BlockSpec(memory_space=pltpu.VMEM)
ANYWHERE = pl.BlockSpec(memory_space=pl.ANY)


def low_array(*shape):
    return jax.ShapeDtypeStruct(shape, jnp.bfloat16)


def moved(byte_count):
    return pl.CostEstimate(flops=0, bytes_accessed=byte_count, transcendentals=0)


def dot_nt(a, b):
    return lax.dot_general(a, b, (((1,), (1,)), ((), ())), preferred_element_type=jnp.float32)


def dot_nn(a, b):
    return lax.dot_general(a, b, (((1,), (0,)), ((), ())), preferred_element_type=jnp.float32)


def dot_tn(a, b):
    return lax.dot_general(a, b, (((0,), (0,)), ((), ())), preferred_element_type=jnp.float32)


def pack_kernel(owners, *refs):
    ins, out_ref = refs[:4], refs[4]
    for owner in range(owners):
        for which in range(4):
            out_ref[owner, 0, which] = ins[which][:, owner * HEAD_DIM : (owner + 1) * HEAD_DIM]


def pack(inputs, chans, turns, turn):
    rows, width = inputs[0].shape
    owners = width // HEAD_DIM // chans // turns
    return pl.pallas_call(
        functools.partial(pack_kernel, owners),
        grid=(chans,),
        out_shape=low_array(owners, chans, 4, rows, HEAD_DIM),
        in_specs=[pl.BlockSpec((rows, owners * HEAD_DIM), lambda c: (0, c * turns + turn))] * 4,
        out_specs=pl.BlockSpec((owners, 1, 4, rows, HEAD_DIM), lambda c: (0, c, 0, 0, 0)),
        cost_estimate=moved(16 * rows * width // turns),
    )(*inputs)


def attention_kernel(spans, count_ref, start_ref, target_ref, source_ref, *refs):
    outs, (in_ref, mixed_ref, key_acc, value_acc, sem) = refs[:-5], refs[-5:]
    blocks, _, block, _ = mixed_ref.shape
    load = pltpu.make_async_copy(source_ref, in_ref, sem)
    load.start()
    key_acc[...] = jnp.zeros_like(key_acc)
    value_acc[...] = jnp.zeros_like(value_acc)
    load.wait()

    def tokens(which, first, count):
        return in_ref[pl.ds(first, count), :, which].reshape(count * block, HEAD_DIM)

    def work(i, span):
        low = i - (span - 1)
        width = span * block
        query = tokens(0, i, 1)
        cot = tokens(3, i, 1).astype(jnp.float32)
        key = tokens(1, low, span)
        value = tokens(2, low, span)
        start = start_ref[pl.ds(pl.multiple_of(i * block, block), block), :] - low * block
        half = block // 2
        expos, cots, dscores = [], [], []
        for first in (0, half):
            part = slice(first, first + half)
            begin = start[part]
            col = lax.broadcasted_iota(jnp.int32, (half, block), 1) + (width - block)
            row = lax.broadcasted_iota(jnp.int32, (half, block), 0) + (width - block + first)
            diagonal = dot_nt(query[part], key[width - block :])
            score = jnp.where((col >= begin) & (col <= row), diagonal, NEG)
            if span > 1:
                col = lax.broadcasted_iota(jnp.int32, (half, width - block), 1)
                before = dot_nt(query[part], key[: width - block])
                score = jnp.concatenate([jnp.where(col >= begin, before, NEG), score], axis=1)
            peak = jnp.max(score, axis=1, keepdims=True)
            expo = jnp.exp2((score - peak) * EXP_SCALE)
            inverse = 1.0 / jnp.sum(expo, axis=1, keepdims=True)
            expo_low = expo.astype(jnp.bfloat16)
            mixed = dot_nn(expo_low, value) * inverse
            scaled = cot[part] * inverse
            scaled_low = scaled.astype(jnp.bfloat16)
            rowdot = jnp.sum(mixed * scaled, axis=1, keepdims=True)
            dscore = (expo * (dot_nt(scaled_low, value) - rowdot)).astype(jnp.bfloat16)
            mixed_ref[i, 0, part] = mixed.astype(jnp.bfloat16)
            mixed_ref[i, 1, part] = (SCALE * dot_nn(dscore, key)).astype(jnp.bfloat16)
            expos.append(expo_low)
            cots.append(scaled_low)
            dscores.append(dscore)
        held = pl.ds(pl.multiple_of(low * block, block), width)
        key_acc[held, :] += dot_tn(jnp.concatenate(dscores, axis=0), query)
        value_acc[held, :] += dot_tn(
            jnp.concatenate(expos, axis=0), jnp.concatenate(cots, axis=0)
        )

    def step(i, carry):
        for span in range(1, spans + 1):
            pl.when(count_ref[i] == span)(functools.partial(work, i, span))
        return carry

    lax.fori_loop(0, blocks, step, 0)
    for d, out_ref in enumerate(outs):
        i = target_ref[d]
        held = pl.ds(pl.multiple_of(i * block, block), block)
        out_ref[:2] = mixed_ref[i]
        out_ref[2] = (SCALE * key_acc[held, :]).astype(jnp.bfloat16)
        out_ref[3] = value_acc[held, :].astype(jnp.bfloat16)


def attention(count, start, targets, packed):
    shards, chans, _, rows, _ = packed.shape
    block = chans * rows
    total = shards * block
    spans = min(shards, (DOC_MAX + block - 2) // block + 1)
    pairs = total * block * min(spans, 3)
    return pl.pallas_call(
        functools.partial(attention_kernel, spans),
        out_shape=[low_array(4, block, HEAD_DIM)] * shards,
        in_specs=[SCALARS, VECTORS, SCALARS, pl.BlockSpec(memory_space=pltpu.HBM)],
        out_specs=[VECTORS] * shards,
        scratch_shapes=[
            pltpu.VMEM(packed.shape, jnp.bfloat16),
            pltpu.VMEM((shards, 2, block, HEAD_DIM), jnp.bfloat16),
            pltpu.VMEM((total, HEAD_DIM), jnp.float32),
            pltpu.VMEM((total, HEAD_DIM), jnp.float32),
            pltpu.SemaphoreType.DMA,
        ],
        compiler_params=pltpu.CompilerParams(vmem_limit_bytes=(16 << 20) + 3840 * total),
        cost_estimate=pl.CostEstimate(
            flops=12 * HEAD_DIM * pairs, bytes_accessed=16 * total * HEAD_DIM, transcendentals=pairs
        ),
    )(count, start, targets, packed)


def unpack_kernel(count, column_ref, *refs):
    blocks, outs, sems = refs[:count], refs[-5:-1], refs[-1]
    moves = []
    for b in range(count):
        columns = pl.ds(pl.multiple_of(column_ref[b] * HEAD_DIM, HEAD_DIM), HEAD_DIM)
        for which in range(4):
            moves.append(
                pltpu.make_async_copy(
                    blocks[b].at[which], outs[which].at[:, columns], sems.at[b, which]
                )
            )
    for move in moves:
        move.start()
    for move in moves:
        move.wait()


def unpack(blocks, columns, width, held):
    count = len(blocks)
    rows = blocks[0].shape[1]
    return pl.pallas_call(
        functools.partial(unpack_kernel, count),
        out_shape=[low_array(rows, width)] * 4,
        in_specs=[SCALARS] + [VECTORS] * count + [ANYWHERE] * len(held),
        out_specs=[ANYWHERE] * 4,
        scratch_shapes=[pltpu.SemaphoreType.DMA((count, 4))],
        input_output_aliases={1 + count + i: i for i in range(len(held))},
        compiler_params=pltpu.CompilerParams(vmem_limit_bytes=16 << 20),
        cost_estimate=moved(16 * count * rows * HEAD_DIM),
    )(columns, *blocks, *held)


def exchange(value, d):
    return lax.ppermute(value, "seq", [(s, s ^ d) for s in range(lax.axis_size("seq"))])


def on_device(doc_ids, *inputs):
    shards = lax.axis_size("seq")
    chans = lax.axis_size("chan")
    rows, width = inputs[0].shape
    heads = width // HEAD_DIM // chans
    turns = max(1, heads // shards)
    owners = heads // turns
    copies = shards // owners
    block = rows * chans
    start = jnp.sum((doc_ids[None, :] < doc_ids[:, None]).astype(jnp.int32), axis=1)
    count = jnp.arange(shards, dtype=jnp.int32) - start[::block] // block + 1
    start = start[:, None]
    peers = jnp.bitwise_xor(lax.axis_index("seq"), jnp.arange(shards, dtype=jnp.int32))
    tied = lax.optimization_barrier

    def gather(parts):
        parts = jnp.repeat(parts, copies, axis=0) if copies > 1 else parts
        parts = parts.reshape(shards * chans, 4, rows, HEAD_DIM)
        parts = lax.all_to_all(parts, ("seq", "chan"), split_axis=0, concat_axis=0, tiled=True)
        return parts.reshape(shards, chans, 4, rows, HEAD_DIM)

    parts = [pack(inputs, chans, turns, turn) for turn in range(turns)]
    later, count, start = tied((parts[1:], count, start))
    mine, parts = tied((gather(parts[0]), later))
    outs, blocks = (), ()
    for turn in range(turns):
        following = gather(parts[turn]) if turn + 1 < turns else None
        mine, blocks = tied((mine, blocks))
        if turn > 0:
            outs = unpack(blocks, columns, heads * HEAD_DIM, outs)
        blocks = list(attention(count, start, peers, mine))
        if copies == 1:
            blocks = [blocks[0]] + [exchange(blocks[d], d) for d in range(1, shards)]
            columns = peers + turn * owners
        else:
            order = jnp.stack(blocks)[peers]
            order = lax.all_to_all(order, "seq", split_axis=0, concat_axis=0, tiled=True)
            blocks = [order[owner * copies] for owner in range(owners)]
            columns = jnp.arange(owners, dtype=jnp.int32)
        mine = following
    return tuple(unpack(blocks, columns, heads * HEAD_DIM, outs))


def solution(mesh):
    spread = P(("seq", "chan"), None)
    in_specs = (P(), spread, spread, spread, spread)
    out_specs = (P("seq", "chan"),) * 4
    return jax.shard_map(
        on_device, mesh=mesh, in_specs=in_specs, out_specs=out_specs, check_vma=False
    )
```

```python
import functools
import math

import jax
import jax.numpy as jnp
from jax import lax
from jax.experimental import pallas as pl
from jax.experimental.pallas import tpu as pltpu
from jax.sharding import PartitionSpec as P

HEAD_DIM = 128
DOC_MAX = 1024
NEG = -1e30
SCALE = HEAD_DIM ** (-0.5)
EXP_SCALE = SCALE * math.log2(math.e)
SCALARS = pl.BlockSpec(memory_space=pltpu.SMEM)
VECTORS = pl.BlockSpec(memory_space=pltpu.VMEM)
ANYWHERE = pl.BlockSpec(memory_space=pl.ANY)


def low_array(*shape):
    return jax.ShapeDtypeStruct(shape, jnp.bfloat16)


def moved(byte_count):
    return pl.CostEstimate(flops=0, bytes_accessed=byte_count, transcendentals=0)


def dot_nt(a, b):
    return lax.dot_general(a, b, (((1,), (1,)), ((), ())), preferred_element_type=jnp.float32)


def dot_nn(a, b):
    return lax.dot_general(a, b, (((1,), (0,)), ((), ())), preferred_element_type=jnp.float32)


def dot_tn(a, b):
    return lax.dot_general(a, b, (((0,), (0,)), ((), ())), preferred_element_type=jnp.float32)


def pack_kernel(owners, *refs):
    ins, out_ref = refs[:4], refs[4]
    for owner in range(owners):
        for which in range(4):
            out_ref[owner, 0, which] = ins[which][:, owner * HEAD_DIM : (owner + 1) * HEAD_DIM]


def pack(inputs, chans, turns, turn):
    rows, width = inputs[0].shape
    owners = width // HEAD_DIM // chans // turns
    return pl.pallas_call(
        functools.partial(pack_kernel, owners),
        grid=(chans, 2),
        out_shape=low_array(owners, chans, 4, rows, HEAD_DIM),
        in_specs=[pl.BlockSpec((rows // 2, owners * HEAD_DIM), lambda c, r: (r, c * turns + turn))]
        * 4,
        out_specs=pl.BlockSpec((owners, 1, 4, rows // 2, HEAD_DIM), lambda c, r: (0, c, 0, r, 0)),
        cost_estimate=moved(16 * rows * width // turns),
    )(*inputs)


def attention_kernel(spans, count_ref, start_ref, target_ref, in_ref, *refs):
    outs, (mixed_ref, key_acc, value_acc) = refs[:-3], refs[-3:]
    blocks, _, block, _ = mixed_ref.shape
    key_acc[...] = jnp.zeros_like(key_acc)
    value_acc[...] = jnp.zeros_like(value_acc)

    def tokens(which, first, count):
        return in_ref[pl.ds(first, count), :, which].reshape(count * block, HEAD_DIM)

    def work(i, span):
        low = i - (span - 1)
        width = span * block
        query = tokens(0, i, 1)
        cot = tokens(3, i, 1).astype(jnp.float32)
        key = tokens(1, low, span)
        value = tokens(2, low, span)
        start = start_ref[pl.ds(pl.multiple_of(i * block, block), block), :] - low * block
        col = lax.broadcasted_iota(jnp.int32, (block, width), 1)
        row = lax.broadcasted_iota(jnp.int32, (block, width), 0) + (span - 1) * block
        allowed = (col >= start) & (col <= row)
        score = jnp.where(allowed, dot_nt(query, key), NEG)
        peak = jnp.max(score, axis=1, keepdims=True)
        expo = jnp.exp2((score - peak) * EXP_SCALE)
        inverse = 1.0 / jnp.sum(expo, axis=1, keepdims=True)
        expo_low = expo.astype(jnp.bfloat16)
        mixed = dot_nn(expo_low, value) * inverse
        scaled = cot * inverse
        scaled_low = scaled.astype(jnp.bfloat16)
        rowdot = jnp.sum(mixed * scaled, axis=1, keepdims=True)
        dscore = (expo * (dot_nt(scaled_low, value) - rowdot)).astype(jnp.bfloat16)
        mixed_ref[i, 0] = mixed.astype(jnp.bfloat16)
        mixed_ref[i, 1] = (SCALE * dot_nn(dscore, key)).astype(jnp.bfloat16)
        held = pl.ds(pl.multiple_of(low * block, block), width)
        key_acc[held, :] += dot_tn(dscore, query)
        value_acc[held, :] += dot_tn(expo_low, scaled_low)

    def step(i, carry):
        for span in range(1, spans + 1):
            pl.when(count_ref[i] == span)(functools.partial(work, i, span))
        return carry

    lax.fori_loop(0, blocks, step, 0)
    for d, out_ref in enumerate(outs):
        i = target_ref[d]
        held = pl.ds(pl.multiple_of(i * block, block), block)
        out_ref[:2] = mixed_ref[i]
        out_ref[2] = (SCALE * key_acc[held, :]).astype(jnp.bfloat16)
        out_ref[3] = value_acc[held, :].astype(jnp.bfloat16)


def attention(count, start, targets, packed):
    shards, chans, _, rows, _ = packed.shape
    block = chans * rows
    total = shards * block
    spans = min(shards, (DOC_MAX + block - 2) // block + 1)
    pairs = total * block * min(spans, 3)
    return pl.pallas_call(
        functools.partial(attention_kernel, spans),
        out_shape=[low_array(4, block, HEAD_DIM)] * shards,
        in_specs=[SCALARS, VECTORS, SCALARS, VECTORS],
        out_specs=[VECTORS] * shards,
        scratch_shapes=[
            pltpu.VMEM((shards, 2, block, HEAD_DIM), jnp.bfloat16),
            pltpu.VMEM((total, HEAD_DIM), jnp.float32),
            pltpu.VMEM((total, HEAD_DIM), jnp.float32),
        ],
        compiler_params=pltpu.CompilerParams(vmem_limit_bytes=(10 << 20) + 3072 * total),
        cost_estimate=pl.CostEstimate(
            flops=12 * HEAD_DIM * pairs, bytes_accessed=16 * total * HEAD_DIM, transcendentals=pairs
        ),
    )(count, start, targets, packed)


def unpack_kernel(peers, base, shard_ref, *refs):
    blocks, outs, sems = refs[: len(peers)], refs[-5:-1], refs[-1]
    moves = []
    for b, d in enumerate(peers):
        head = base + jnp.bitwise_xor(shard_ref[0], d)
        columns = pl.ds(pl.multiple_of(head * HEAD_DIM, HEAD_DIM), HEAD_DIM)
        for which in range(4):
            moves.append(
                pltpu.make_async_copy(
                    blocks[b].at[which], outs[which].at[:, columns], sems.at[b, which]
                )
            )
    for move in moves:
        move.start()
    for move in moves:
        move.wait()


def unpack(shard, blocks, peers, base, width, held):
    count = len(blocks)
    rows = blocks[0].shape[1]
    return pl.pallas_call(
        functools.partial(unpack_kernel, peers, base),
        out_shape=[low_array(rows, width)] * 4,
        in_specs=[SCALARS] + [VECTORS] * count + [ANYWHERE] * len(held),
        out_specs=[ANYWHERE] * 4,
        scratch_shapes=[pltpu.SemaphoreType.DMA((count, 4))],
        input_output_aliases={1 + count + i: i for i in range(len(held))},
        compiler_params=pltpu.CompilerParams(vmem_limit_bytes=8 << 20),
        cost_estimate=moved(16 * count * rows * HEAD_DIM),
    )(shard, *blocks, *held)


def exchange(value, d):
    return lax.ppermute(value, "seq", [(s, s ^ d) for s in range(lax.axis_size("seq"))])


def on_device(doc_ids, *inputs):
    shards = lax.axis_size("seq")
    chans = lax.axis_size("chan")
    rows, width = inputs[0].shape
    heads = width // HEAD_DIM // chans
    turns = max(1, heads // shards)
    owners = heads // turns
    copies = shards // owners
    block = rows * chans
    start = jnp.sum((doc_ids[None, :] < doc_ids[:, None]).astype(jnp.int32), axis=1)
    count = jnp.arange(shards, dtype=jnp.int32) - start[::block] // block + 1
    start = start[:, None]
    peers = jnp.bitwise_xor(lax.axis_index("seq"), jnp.arange(shards, dtype=jnp.int32))
    tied = lax.optimization_barrier

    def gather(parts):
        parts = jnp.repeat(parts, copies, axis=0) if copies > 1 else parts
        parts = parts.reshape(shards * chans, 4, rows, HEAD_DIM)
        parts = lax.all_to_all(parts, ("seq", "chan"), split_axis=0, concat_axis=0, tiled=True)
        return parts.reshape(shards, chans, 4, rows, HEAD_DIM)

    parts = [pack(inputs, chans, turns, turn) for turn in range(turns)]
    later, count, start = tied((parts[1:], count, start))
    mine, parts = tied((gather(parts[0]), later))
    order = [0] + sorted(range(1, shards), key=lambda d: (-(d >> 1).bit_count(), d & 1, d))
    outs, blocks = (), ()
    for turn in range(turns):
        following = gather(parts[turn]) if turn + 1 < turns else None
        mine, blocks = tied((mine, blocks))
        if turn > 0:
            outs = unpack(place, blocks, order, (turn - 1) * owners, heads * HEAD_DIM, outs)
        blocks = list(attention(count, start, peers, mine))
        if copies == 1:
            blocks = [exchange(blocks[d], d) if d else blocks[d] for d in order]
            place = lax.axis_index("seq")[None]
        else:
            whole = jnp.stack(blocks)[peers]
            whole = lax.all_to_all(whole, "seq", split_axis=0, concat_axis=0, tiled=True)
            blocks = [whole[owner * copies] for owner in range(owners)]
            place, order = jnp.zeros((1,), jnp.int32), list(range(owners))
        mine = following
    early, base = len(blocks) // 2 + 1, (turns - 1) * owners
    outs = unpack(place, blocks[:early], order[:early], base, heads * HEAD_DIM, outs)
    return tuple(unpack(place, blocks[early:], order[early:], base, heads * HEAD_DIM, outs))


def solution(mesh):
    spread = P(("seq", "chan"), None)
    in_specs = (P(), spread, spread, spread, spread)
    out_specs = (P("seq", "chan"),) * 4
    return jax.shard_map(
        on_device, mesh=mesh, in_specs=in_specs, out_specs=out_specs, check_vma=False
    )
```

```python
import functools
import math

import jax
import jax.numpy as jnp
from jax import lax
from jax.experimental import pallas as pl
from jax.experimental.pallas import tpu as pltpu
from jax.sharding import PartitionSpec as P

HEAD_DIM = 128
DOC_MAX = 1024
NEG = -1e30
SCALE = HEAD_DIM ** (-0.5)
EXP_SCALE = SCALE * math.log2(math.e)
SCALARS = pl.BlockSpec(memory_space=pltpu.SMEM)
VECTORS = pl.BlockSpec(memory_space=pltpu.VMEM)
ANYWHERE = pl.BlockSpec(memory_space=pl.ANY)


def low_array(*shape):
    return jax.ShapeDtypeStruct(shape, jnp.bfloat16)


def moved(byte_count):
    return pl.CostEstimate(flops=0, bytes_accessed=byte_count, transcendentals=0)


def dot_nt(a, b):
    return lax.dot_general(a, b, (((1,), (1,)), ((), ())), preferred_element_type=jnp.float32)


def dot_nn(a, b):
    return lax.dot_general(a, b, (((1,), (0,)), ((), ())), preferred_element_type=jnp.float32)


def dot_tn(a, b):
    return lax.dot_general(a, b, (((0,), (0,)), ((), ())), preferred_element_type=jnp.float32)


def pack_kernel(owners, chans, *refs):
    ins, out_ref = refs[:-1], refs[-1]
    for chan in range(chans):
        for owner in range(owners):
            for which in range(4):
                columns = slice(owner * HEAD_DIM, (owner + 1) * HEAD_DIM)
                out_ref[owner, chan, which] = ins[4 * chan + which][:, columns]


def pack(inputs, chans, turns, turn):
    rows, width = inputs[0].shape
    owners = width // HEAD_DIM // chans // turns

    def columns(chan):
        return pl.BlockSpec((rows, owners * HEAD_DIM), lambda i: (0, chan * turns + turn))

    return pl.pallas_call(
        functools.partial(pack_kernel, owners, chans),
        grid=(1,),
        out_shape=low_array(owners, chans, 4, rows, HEAD_DIM),
        in_specs=[columns(chan) for chan in range(chans) for _ in range(4)],
        out_specs=pl.BlockSpec((owners, chans, 4, rows, HEAD_DIM), lambda i: (0, 0, 0, 0, 0)),
        compiler_params=pltpu.CompilerParams(vmem_limit_bytes=20 << 20),
        cost_estimate=moved(16 * rows * width // turns),
    )(*(list(inputs) * chans))


def attention_kernel(spans, count_ref, start_ref, target_ref, in_ref, *refs):
    outs, (mixed_ref, key_acc, value_acc) = refs[:-3], refs[-3:]
    blocks, _, block, _ = mixed_ref.shape
    key_acc[...] = jnp.zeros_like(key_acc)
    value_acc[...] = jnp.zeros_like(value_acc)

    def tokens(which, first, count):
        return in_ref[pl.ds(first, count), :, which].reshape(count * block, HEAD_DIM)

    def work(i, span):
        low = i - (span - 1)
        width = span * block
        query = tokens(0, i, 1)
        cot = tokens(3, i, 1).astype(jnp.float32)
        key = tokens(1, low, span)
        value = tokens(2, low, span)
        start = start_ref[pl.ds(pl.multiple_of(i * block, block), block), :] - low * block
        col = lax.broadcasted_iota(jnp.int32, (block, width), 1)
        row = lax.broadcasted_iota(jnp.int32, (block, width), 0) + (span - 1) * block
        allowed = (col >= start) & (col <= row)
        score = jnp.where(allowed, dot_nt(query, key), NEG)
        peak = jnp.max(score, axis=1, keepdims=True)
        expo = jnp.exp2((score - peak) * EXP_SCALE)
        inverse = 1.0 / jnp.sum(expo, axis=1, keepdims=True)
        expo_low = expo.astype(jnp.bfloat16)
        mixed = dot_nn(expo_low, value) * inverse
        scaled = cot * inverse
        scaled_low = scaled.astype(jnp.bfloat16)
        rowdot = jnp.sum(mixed * scaled, axis=1, keepdims=True)
        dscore = (expo * (dot_nt(scaled_low, value) - rowdot)).astype(jnp.bfloat16)
        mixed_ref[i, 0] = mixed.astype(jnp.bfloat16)
        mixed_ref[i, 1] = (SCALE * dot_nn(dscore, key)).astype(jnp.bfloat16)
        held = pl.ds(pl.multiple_of(low * block, block), width)
        key_acc[held, :] += dot_tn(dscore, query)
        value_acc[held, :] += dot_tn(expo_low, scaled_low)

    def step(i, carry):
        for span in range(1, spans + 1):
            pl.when(count_ref[i] == span)(functools.partial(work, i, span))
        return carry

    lax.fori_loop(0, blocks, step, 0)
    for d, out_ref in enumerate(outs):
        i = target_ref[d]
        held = pl.ds(pl.multiple_of(i * block, block), block)
        out_ref[:2] = mixed_ref[i]
        out_ref[2] = (SCALE * key_acc[held, :]).astype(jnp.bfloat16)
        out_ref[3] = value_acc[held, :].astype(jnp.bfloat16)


def attention(count, start, targets, packed):
    shards, chans, _, rows, _ = packed.shape
    block = chans * rows
    total = shards * block
    spans = min(shards, (DOC_MAX + block - 2) // block + 1)
    pairs = total * block * min(spans, 3)
    return pl.pallas_call(
        functools.partial(attention_kernel, spans),
        out_shape=[low_array(4, block, HEAD_DIM)] * shards,
        in_specs=[SCALARS, VECTORS, SCALARS, VECTORS],
        out_specs=[VECTORS] * shards,
        scratch_shapes=[
            pltpu.VMEM((shards, 2, block, HEAD_DIM), jnp.bfloat16),
            pltpu.VMEM((total, HEAD_DIM), jnp.float32),
            pltpu.VMEM((total, HEAD_DIM), jnp.float32),
        ],
        compiler_params=pltpu.CompilerParams(vmem_limit_bytes=(10 << 20) + 3072 * total),
        cost_estimate=pl.CostEstimate(
            flops=12 * HEAD_DIM * pairs, bytes_accessed=16 * total * HEAD_DIM, transcendentals=pairs
        ),
    )(count, start, targets, packed)


def unpack_kernel(peers, base, shard_ref, *refs):
    blocks, outs, sems = refs[: len(peers)], refs[-5:-1], refs[-1]
    moves = []
    for b, d in enumerate(peers):
        head = base + jnp.bitwise_xor(shard_ref[0], d)
        columns = pl.ds(pl.multiple_of(head * HEAD_DIM, HEAD_DIM), HEAD_DIM)
        for which in range(4):
            moves.append(
                pltpu.make_async_copy(
                    blocks[b].at[which], outs[which].at[:, columns], sems.at[b, which]
                )
            )
    for move in moves:
        move.start()
    for move in moves:
        move.wait()


def unpack(shard, blocks, peers, base, width, held):
    count = len(blocks)
    rows = blocks[0].shape[1]
    return pl.pallas_call(
        functools.partial(unpack_kernel, peers, base),
        out_shape=[low_array(rows, width)] * 4,
        in_specs=[SCALARS] + [VECTORS] * count + [ANYWHERE] * len(held),
        out_specs=[ANYWHERE] * 4,
        scratch_shapes=[pltpu.SemaphoreType.DMA((count, 4))],
        input_output_aliases={1 + count + i: i for i in range(len(held))},
        compiler_params=pltpu.CompilerParams(vmem_limit_bytes=8 << 20),
        cost_estimate=moved(16 * count * rows * HEAD_DIM),
    )(shard, *blocks, *held)


def exchange(value, d):
    return lax.ppermute(value, "seq", [(s, s ^ d) for s in range(lax.axis_size("seq"))])


def on_device(doc_ids, *inputs):
    shards = lax.axis_size("seq")
    chans = lax.axis_size("chan")
    rows, width = inputs[0].shape
    heads = width // HEAD_DIM // chans
    turns = max(1, heads // shards)
    owners = heads // turns
    copies = shards // owners
    block = rows * chans
    start = jnp.sum((doc_ids[None, :] < doc_ids[:, None]).astype(jnp.int32), axis=1)
    count = jnp.arange(shards, dtype=jnp.int32) - start[::block] // block + 1
    start = start[:, None]
    peers = jnp.bitwise_xor(lax.axis_index("seq"), jnp.arange(shards, dtype=jnp.int32))
    tied = lax.optimization_barrier

    def gather(parts):
        parts = jnp.repeat(parts, copies, axis=0) if copies > 1 else parts
        parts = parts.reshape(shards * chans, 4, rows, HEAD_DIM)
        parts = lax.all_to_all(parts, ("seq", "chan"), split_axis=0, concat_axis=0, tiled=True)
        return parts.reshape(shards, chans, 4, rows, HEAD_DIM)

    parts = [pack(inputs, chans, turns, turn) for turn in range(turns)]
    later, count, start = tied((parts[1:], count, start))
    mine, parts = tied((gather(parts[0]), later))
    order = [0] + sorted(range(1, shards), key=lambda d: (-(d >> 1).bit_count(), d & 1, d))
    outs, blocks = (), ()
    for turn in range(turns):
        following = gather(parts[turn]) if turn + 1 < turns else None
        mine, outs = tied((mine, outs))
        blocks = list(attention(count, start, peers, mine))
        if copies == 1:
            blocks = [exchange(blocks[d], d) if d else blocks[d] for d in order]
            place = lax.axis_index("seq")[None]
        else:
            whole = jnp.stack(blocks)[peers]
            whole = lax.all_to_all(whole, "seq", split_axis=0, concat_axis=0, tiled=True)
            blocks = [whole[owner * copies] for owner in range(owners)]
            place, order = jnp.zeros((1,), jnp.int32), list(range(owners))
        early, base = len(blocks) // 2 + 1, turn * owners
        outs = unpack(place, blocks[:early], order[:early], base, heads * HEAD_DIM, outs)
        outs = unpack(place, blocks[early:], order[early:], base, heads * HEAD_DIM, outs)
        mine = following
    return tuple(outs)


def solution(mesh):
    spread = P(("seq", "chan"), None)
    in_specs = (P(), spread, spread, spread, spread)
    out_specs = (P("seq", "chan"),) * 4
    return jax.shard_map(
        on_device, mesh=mesh, in_specs=in_specs, out_specs=out_specs, check_vma=False
    )
```

```python
import functools
import math

import jax
import jax.numpy as jnp
from jax import lax
from jax.experimental import pallas as pl
from jax.experimental.pallas import tpu as pltpu
from jax.sharding import PartitionSpec as P

HEAD_DIM = 128
DOC_MAX = 1024
NEG = -1e30
SCALE = HEAD_DIM ** (-0.5)
EXP_SCALE = SCALE * math.log2(math.e)
SCALARS = pl.BlockSpec(memory_space=pltpu.SMEM)
VECTORS = pl.BlockSpec(memory_space=pltpu.VMEM)
ANYWHERE = pl.BlockSpec(memory_space=pl.ANY)


def low_array(*shape):
    return jax.ShapeDtypeStruct(shape, jnp.bfloat16)


def moved(byte_count):
    return pl.CostEstimate(flops=0, bytes_accessed=byte_count, transcendentals=0)


def dot_nt(a, b):
    return lax.dot_general(a, b, (((1,), (1,)), ((), ())), preferred_element_type=jnp.float32)


def dot_nn(a, b):
    return lax.dot_general(a, b, (((1,), (0,)), ((), ())), preferred_element_type=jnp.float32)


def dot_tn(a, b):
    return lax.dot_general(a, b, (((0,), (0,)), ((), ())), preferred_element_type=jnp.float32)


def pack_kernel(owners, *refs):
    ins, out_ref = refs[:4], refs[4]
    for owner in range(owners):
        for which in range(4):
            out_ref[owner, 0, which] = ins[which][:, owner * HEAD_DIM : (owner + 1) * HEAD_DIM]


def pack(inputs, chans, turns, turn):
    rows, width = inputs[0].shape
    owners = width // HEAD_DIM // chans // turns
    return pl.pallas_call(
        functools.partial(pack_kernel, owners),
        grid=(chans,),
        out_shape=low_array(owners, chans, 4, rows, HEAD_DIM),
        in_specs=[pl.BlockSpec((rows, owners * HEAD_DIM), lambda c: (0, c * turns + turn))] * 4,
        out_specs=pl.BlockSpec((owners, 1, 4, rows, HEAD_DIM), lambda c: (0, c, 0, 0, 0)),
        cost_estimate=moved(16 * rows * width // turns),
    )(*inputs)


def attention_kernel(spans, count_ref, start_ref, target_ref, in_ref, *refs):
    outs, (mixed_ref, key_acc, value_acc) = refs[:-3], refs[-3:]
    blocks, _, block, _ = mixed_ref.shape
    key_acc[...] = jnp.zeros_like(key_acc)
    value_acc[...] = jnp.zeros_like(value_acc)

    def tokens(which, first, count):
        return in_ref[pl.ds(first, count), :, which].reshape(count * block, HEAD_DIM)

    def work(i, span):
        low = i - (span - 1)
        width = span * block
        query = tokens(0, i, 1)
        cot = tokens(3, i, 1).astype(jnp.float32)
        key = tokens(1, low, span)
        value = tokens(2, low, span)
        start = start_ref[pl.ds(pl.multiple_of(i * block, block), block), :] - low * block
        col = lax.broadcasted_iota(jnp.int32, (block, width), 1)
        row = lax.broadcasted_iota(jnp.int32, (block, width), 0) + (span - 1) * block
        allowed = (col >= start) & (col <= row)
        score = jnp.where(allowed, dot_nt(query, key), NEG)
        peak = jnp.max(score, axis=1, keepdims=True)
        expo = jnp.exp2((score - peak) * EXP_SCALE)
        inverse = 1.0 / jnp.sum(expo, axis=1, keepdims=True)
        expo_low = expo.astype(jnp.bfloat16)
        mixed = dot_nn(expo_low, value) * inverse
        scaled = cot * inverse
        scaled_low = scaled.astype(jnp.bfloat16)
        rowdot = jnp.sum(mixed * scaled, axis=1, keepdims=True)
        dscore = (expo * (dot_nt(scaled_low, value) - rowdot)).astype(jnp.bfloat16)
        mixed_ref[i, 0] = mixed.astype(jnp.bfloat16)
        mixed_ref[i, 1] = (SCALE * dot_nn(dscore, key)).astype(jnp.bfloat16)
        held = pl.ds(pl.multiple_of(low * block, block), width)
        key_acc[held, :] += dot_tn(dscore, query)
        value_acc[held, :] += dot_tn(expo_low, scaled_low)

    def step(i, carry):
        for span in range(1, spans + 1):
            pl.when(count_ref[i] == span)(functools.partial(work, i, span))
        return carry

    lax.fori_loop(0, blocks, step, 0)
    for d, out_ref in enumerate(outs):
        i = target_ref[d]
        held = pl.ds(pl.multiple_of(i * block, block), block)
        out_ref[:2] = mixed_ref[i]
        out_ref[2] = (SCALE * key_acc[held, :]).astype(jnp.bfloat16)
        out_ref[3] = value_acc[held, :].astype(jnp.bfloat16)


def attention(count, start, targets, packed):
    shards, chans, _, rows, _ = packed.shape
    block = chans * rows
    total = shards * block
    spans = min(shards, (DOC_MAX + block - 2) // block + 1)
    pairs = total * block * min(spans, 3)
    return pl.pallas_call(
        functools.partial(attention_kernel, spans),
        out_shape=[low_array(4, block, HEAD_DIM)] * shards,
        in_specs=[SCALARS, VECTORS, SCALARS, VECTORS],
        out_specs=[VECTORS] * shards,
        scratch_shapes=[
            pltpu.VMEM((shards, 2, block, HEAD_DIM), jnp.bfloat16),
            pltpu.VMEM((total, HEAD_DIM), jnp.float32),
            pltpu.VMEM((total, HEAD_DIM), jnp.float32),
        ],
        compiler_params=pltpu.CompilerParams(vmem_limit_bytes=(10 << 20) + 3072 * total),
        cost_estimate=pl.CostEstimate(
            flops=12 * HEAD_DIM * pairs, bytes_accessed=16 * total * HEAD_DIM, transcendentals=pairs
        ),
    )(count, start, targets, packed)


def unpack_kernel(peers, base, shard_ref, *refs):
    blocks, outs, sems = refs[: len(peers)], refs[-5:-1], refs[-1]
    moves = []
    for b, d in enumerate(peers):
        head = base + jnp.bitwise_xor(shard_ref[0], d)
        columns = pl.ds(pl.multiple_of(head * HEAD_DIM, HEAD_DIM), HEAD_DIM)
        for which in range(4):
            moves.append(
                pltpu.make_async_copy(
                    blocks[b].at[which], outs[which].at[:, columns], sems.at[b, which]
                )
            )
    for move in moves:
        move.start()
    for move in moves:
        move.wait()


def unpack(shard, blocks, peers, base, width, held):
    count = len(blocks)
    rows = blocks[0].shape[1]
    return pl.pallas_call(
        functools.partial(unpack_kernel, peers, base),
        out_shape=[low_array(rows, width)] * 4,
        in_specs=[SCALARS] + [VECTORS] * count + [ANYWHERE] * len(held),
        out_specs=[ANYWHERE] * 4,
        scratch_shapes=[pltpu.SemaphoreType.DMA((count, 4))],
        input_output_aliases={1 + count + i: i for i in range(len(held))},
        compiler_params=pltpu.CompilerParams(vmem_limit_bytes=8 << 20),
        cost_estimate=moved(16 * count * rows * HEAD_DIM),
    )(shard, *blocks, *held)


def exchange(value, d):
    return lax.ppermute(value, "seq", [(s, s ^ d) for s in range(lax.axis_size("seq"))])


def on_device(doc_ids, *inputs):
    shards = lax.axis_size("seq")
    chans = lax.axis_size("chan")
    rows, width = inputs[0].shape
    heads = width // HEAD_DIM // chans
    turns = max(1, heads // shards)
    owners = heads // turns
    copies = shards // owners
    block = rows * chans
    start = jnp.sum((doc_ids[None, :] < doc_ids[:, None]).astype(jnp.int32), axis=1)
    count = jnp.arange(shards, dtype=jnp.int32) - start[::block] // block + 1
    start = start[:, None]
    peers = jnp.bitwise_xor(lax.axis_index("seq"), jnp.arange(shards, dtype=jnp.int32))
    tied = lax.optimization_barrier

    def gather(parts):
        parts = jnp.repeat(parts, copies, axis=0) if copies > 1 else parts
        parts = parts.reshape(shards * chans, 4, rows, HEAD_DIM)
        parts = lax.all_to_all(parts, ("seq", "chan"), split_axis=0, concat_axis=0, tiled=True)
        return parts.reshape(shards, chans, 4, rows, HEAD_DIM)

    parts = [pack(inputs, chans, turns, turn) for turn in range(turns)]
    later, count, start = tied((parts[1:], count, start))
    mine, parts = tied((gather(parts[0]), later))
    order = [0] + sorted(range(1, shards), key=lambda d: (-(d >> 1).bit_count(), d & 1, d))
    outs, blocks = (), ()
    for turn in range(turns):
        following = gather(parts[turn]) if turn + 1 < turns else None
        mine, outs = tied((mine, outs))
        blocks = list(attention(count, start, peers, mine))
        if copies == 1:
            blocks = [exchange(blocks[d], d) if d else blocks[d] for d in order]
            place = lax.axis_index("seq")[None]
        else:
            whole = jnp.stack(blocks)[peers]
            whole = lax.all_to_all(whole, "seq", split_axis=0, concat_axis=0, tiled=True)
            blocks = [whole[owner * copies] for owner in range(owners)]
            place, order = jnp.zeros((1,), jnp.int32), list(range(owners))
        early, base = len(blocks) // 2 + 1, turn * owners
        outs = unpack(place, blocks[:early], order[:early], base, heads * HEAD_DIM, outs)
        outs = unpack(place, blocks[early:], order[early:], base, heads * HEAD_DIM, outs)
        mine = following
    return tuple(outs)


def solution(mesh):
    spread = P(("seq", "chan"), None)
    in_specs = (P(), spread, spread, spread, spread)
    out_specs = (P("seq", "chan"),) * 4
    return jax.shard_map(
        on_device, mesh=mesh, in_specs=in_specs, out_specs=out_specs, check_vma=False
    )
```

```python
import functools
import math

import jax
import jax.numpy as jnp
from jax import lax
from jax.experimental import pallas as pl
from jax.experimental.pallas import tpu as pltpu
from jax.sharding import PartitionSpec as P

HEAD_DIM = 128
DOC_MAX = 1024
NEG = -1e30
SCALE = HEAD_DIM ** (-0.5)
EXP_SCALE = SCALE * math.log2(math.e)
SCALARS = pl.BlockSpec(memory_space=pltpu.SMEM)
VECTORS = pl.BlockSpec(memory_space=pltpu.VMEM)
ANYWHERE = pl.BlockSpec(memory_space=pl.ANY)


def low_array(*shape):
    return jax.ShapeDtypeStruct(shape, jnp.bfloat16)


def moved(byte_count):
    return pl.CostEstimate(flops=0, bytes_accessed=byte_count, transcendentals=0)


def dot_nt(a, b):
    return lax.dot_general(a, b, (((1,), (1,)), ((), ())), preferred_element_type=jnp.float32)


def dot_nn(a, b):
    return lax.dot_general(a, b, (((1,), (0,)), ((), ())), preferred_element_type=jnp.float32)


def dot_tn(a, b):
    return lax.dot_general(a, b, (((0,), (0,)), ((), ())), preferred_element_type=jnp.float32)


def pack_kernel(owners, *refs):
    ins, out_ref = refs[:4], refs[4]
    for owner in range(owners):
        for which in range(4):
            out_ref[owner, 0, which] = ins[which][:, owner * HEAD_DIM : (owner + 1) * HEAD_DIM]


def pack(inputs, chans, turns, turn):
    rows, width = inputs[0].shape
    owners = width // HEAD_DIM // chans // turns
    return pl.pallas_call(
        functools.partial(pack_kernel, owners),
        grid=(chans,),
        out_shape=low_array(owners, chans, 4, rows, HEAD_DIM),
        in_specs=[pl.BlockSpec((rows, owners * HEAD_DIM), lambda c: (0, c * turns + turn))] * 4,
        out_specs=pl.BlockSpec((owners, 1, 4, rows, HEAD_DIM), lambda c: (0, c, 0, 0, 0)),
        compiler_params=pltpu.CompilerParams(vmem_limit_bytes=8 << 20),
        cost_estimate=moved(16 * rows * width // turns),
    )(*inputs)


def attention_kernel(spans, count_ref, start_ref, target_ref, in_ref, *refs):
    outs, (mixed_ref, key_acc, value_acc) = refs[:-3], refs[-3:]
    blocks, _, block, _ = mixed_ref.shape
    key_acc[...] = jnp.zeros_like(key_acc)
    value_acc[...] = jnp.zeros_like(value_acc)

    def tokens(which, first, count):
        return in_ref[pl.ds(first, count), :, which].reshape(count * block, HEAD_DIM)

    def work(i, span):
        low = i - (span - 1)
        width = span * block
        query = tokens(0, i, 1)
        cot = tokens(3, i, 1).astype(jnp.float32)
        key = tokens(1, low, span)
        value = tokens(2, low, span)
        start = start_ref[pl.ds(pl.multiple_of(i * block, block), block), :] - low * block
        col = lax.broadcasted_iota(jnp.int32, (block, width), 1)
        row = lax.broadcasted_iota(jnp.int32, (block, width), 0) + (span - 1) * block
        allowed = (col >= start) & (col <= row)
        score = jnp.where(allowed, dot_nt(query, key), NEG)
        peak = jnp.max(score, axis=1, keepdims=True)
        expo = jnp.exp2((score - peak) * EXP_SCALE)
        inverse = 1.0 / jnp.sum(expo, axis=1, keepdims=True)
        expo_low = expo.astype(jnp.bfloat16)
        mixed = dot_nn(expo_low, value) * inverse
        scaled = cot * inverse
        scaled_low = scaled.astype(jnp.bfloat16)
        rowdot = jnp.sum(mixed * scaled, axis=1, keepdims=True)
        dscore = (expo * (dot_nt(scaled_low, value) - rowdot)).astype(jnp.bfloat16)
        mixed_ref[i, 0] = mixed.astype(jnp.bfloat16)
        mixed_ref[i, 1] = (SCALE * dot_nn(dscore, key)).astype(jnp.bfloat16)
        held = pl.ds(pl.multiple_of(low * block, block), width)
        key_acc[held, :] += dot_tn(dscore, query)
        value_acc[held, :] += dot_tn(expo_low, scaled_low)

    def step(i, carry):
        for span in range(1, spans + 1):
            pl.when(count_ref[i] == span)(functools.partial(work, i, span))
        return carry

    lax.fori_loop(0, blocks, step, 0)
    for d, out_ref in enumerate(outs):
        i = target_ref[d]
        held = pl.ds(pl.multiple_of(i * block, block), block)
        out_ref[:2] = mixed_ref[i]
        out_ref[2] = (SCALE * key_acc[held, :]).astype(jnp.bfloat16)
        out_ref[3] = value_acc[held, :].astype(jnp.bfloat16)


def attention(count, start, targets, packed):
    shards, chans, _, rows, _ = packed.shape
    block = chans * rows
    total = shards * block
    spans = min(shards, (DOC_MAX + block - 2) // block + 1)
    pairs = total * block * min(spans, 3)
    return pl.pallas_call(
        functools.partial(attention_kernel, spans),
        out_shape=[low_array(4, block, HEAD_DIM)] * shards,
        in_specs=[SCALARS, VECTORS, SCALARS, VECTORS],
        out_specs=[VECTORS] * shards,
        scratch_shapes=[
            pltpu.VMEM((shards, 2, block, HEAD_DIM), jnp.bfloat16),
            pltpu.VMEM((total, HEAD_DIM), jnp.float32),
            pltpu.VMEM((total, HEAD_DIM), jnp.float32),
        ],
        compiler_params=pltpu.CompilerParams(vmem_limit_bytes=(10 << 20) + 3072 * total),
        cost_estimate=pl.CostEstimate(
            flops=12 * HEAD_DIM * pairs, bytes_accessed=16 * total * HEAD_DIM, transcendentals=pairs
        ),
    )(count, start, targets, packed)


def unpack_kernel(peers, base, shard_ref, *refs):
    blocks, outs, sems = refs[: len(peers)], refs[-5:-1], refs[-1]
    moves = []
    for b, d in enumerate(peers):
        head = base + jnp.bitwise_xor(shard_ref[0], d)
        columns = pl.ds(pl.multiple_of(head * HEAD_DIM, HEAD_DIM), HEAD_DIM)
        for which in range(4):
            moves.append(
                pltpu.make_async_copy(
                    blocks[b].at[which], outs[which].at[:, columns], sems.at[b, which]
                )
            )
    for move in moves:
        move.start()
    for move in moves:
        move.wait()


def unpack(shard, blocks, peers, base, width, held):
    count = len(blocks)
    rows = blocks[0].shape[1]
    return pl.pallas_call(
        functools.partial(unpack_kernel, peers, base),
        out_shape=[low_array(rows, width)] * 4,
        in_specs=[SCALARS] + [VECTORS] * count + [ANYWHERE] * len(held),
        out_specs=[ANYWHERE] * 4,
        scratch_shapes=[pltpu.SemaphoreType.DMA((count, 4))],
        input_output_aliases={1 + count + i: i for i in range(len(held))},
        compiler_params=pltpu.CompilerParams(vmem_limit_bytes=8 << 20),
        cost_estimate=moved(16 * count * rows * HEAD_DIM),
    )(shard, *blocks, *held)


def exchange(value, d):
    return lax.ppermute(value, "seq", [(s, s ^ d) for s in range(lax.axis_size("seq"))])


def on_device(doc_ids, *inputs):
    shards = lax.axis_size("seq")
    chans = lax.axis_size("chan")
    rows, width = inputs[0].shape
    heads = width // HEAD_DIM // chans
    turns = max(1, heads // shards)
    owners = heads // turns
    copies = shards // owners
    block = rows * chans
    start = jnp.sum((doc_ids[None, :] < doc_ids[:, None]).astype(jnp.int32), axis=1)
    count = jnp.arange(shards, dtype=jnp.int32) - start[::block] // block + 1
    start = start[:, None]
    peers = jnp.bitwise_xor(lax.axis_index("seq"), jnp.arange(shards, dtype=jnp.int32))
    tied = lax.optimization_barrier

    def gather(parts):
        parts = jnp.repeat(parts, copies, axis=0) if copies > 1 else parts
        parts = parts.reshape(shards * chans, 4, rows, HEAD_DIM)
        parts = lax.all_to_all(parts, ("seq", "chan"), split_axis=0, concat_axis=0, tiled=True)
        return parts.reshape(shards, chans, 4, rows, HEAD_DIM)

    parts = [pack(inputs, chans, turns, turn) for turn in range(turns)]
    later, count, start = tied((parts[1:], count, start))
    mine, parts = tied((gather(parts[0]), later))
    order = [0] + sorted(range(1, shards), key=lambda d: (-(d >> 1).bit_count(), d & 1, d))
    outs, blocks = (), ()
    for turn in range(turns):
        following = gather(parts[turn]) if turn + 1 < turns else None
        mine, outs = tied((mine, outs))
        blocks = list(attention(count, start, peers, mine))
        if copies == 1:
            blocks = [exchange(blocks[d], d) if d else blocks[d] for d in order]
            place = lax.axis_index("seq")[None]
        else:
            whole = jnp.stack(blocks)[peers]
            whole = lax.all_to_all(whole, "seq", split_axis=0, concat_axis=0, tiled=True)
            blocks = [whole[owner * copies] for owner in range(owners)]
            place, order = jnp.zeros((1,), jnp.int32), list(range(owners))
        early, base = len(blocks) // 2 + 1, turn * owners
        outs = unpack(place, blocks[:early], order[:early], base, heads * HEAD_DIM, outs)
        outs = unpack(place, blocks[early:], order[early:], base, heads * HEAD_DIM, outs)
        mine = following
    return tuple(outs)


def solution(mesh):
    spread = P(("seq", "chan"), None)
    in_specs = (P(), spread, spread, spread, spread)
    out_specs = (P("seq", "chan"),) * 4
    return jax.shard_map(
        on_device, mesh=mesh, in_specs=in_specs, out_specs=out_specs, check_vma=False
    )
```

```python
import functools
import math

import jax
import jax.numpy as jnp
from jax import lax
from jax.experimental import pallas as pl
from jax.experimental.pallas import tpu as pltpu
from jax.sharding import PartitionSpec as P

HEAD_DIM = 128
DOC_MAX = 1024
NEG = -1e30
SCALE = HEAD_DIM ** (-0.5)
EXP_SCALE = SCALE * math.log2(math.e)
SCALARS = pl.BlockSpec(memory_space=pltpu.SMEM)
VECTORS = pl.BlockSpec(memory_space=pltpu.VMEM)
ANYWHERE = pl.BlockSpec(memory_space=pl.ANY)


def low_array(*shape):
    return jax.ShapeDtypeStruct(shape, jnp.bfloat16)


def moved(byte_count):
    return pl.CostEstimate(flops=0, bytes_accessed=byte_count, transcendentals=0)


def dot_nt(a, b):
    return lax.dot_general(a, b, (((1,), (1,)), ((), ())), preferred_element_type=jnp.float32)


def dot_nn(a, b):
    return lax.dot_general(a, b, (((1,), (0,)), ((), ())), preferred_element_type=jnp.float32)


def dot_tn(a, b):
    return lax.dot_general(a, b, (((0,), (0,)), ((), ())), preferred_element_type=jnp.float32)


def pack_kernel(owners, *refs):
    ins, out_ref = refs[:4], refs[4]
    for owner in range(owners):
        for which in range(4):
            out_ref[owner, 0, which] = ins[which][:, owner * HEAD_DIM : (owner + 1) * HEAD_DIM]


def pack(inputs, chans, turns, turn):
    rows, width = inputs[0].shape
    owners = width // HEAD_DIM // chans // turns
    return pl.pallas_call(
        functools.partial(pack_kernel, owners),
        grid=(chans,),
        out_shape=low_array(owners, chans, 4, rows, HEAD_DIM),
        in_specs=[pl.BlockSpec((rows, owners * HEAD_DIM), lambda c: (0, c * turns + turn))] * 4,
        out_specs=pl.BlockSpec((owners, 1, 4, rows, HEAD_DIM), lambda c: (0, c, 0, 0, 0)),
        compiler_params=pltpu.CompilerParams(vmem_limit_bytes=8 << 20) if turn else None,
        cost_estimate=moved(16 * rows * width // turns),
    )(*inputs)


def attention_kernel(spans, count_ref, start_ref, target_ref, in_ref, *refs):
    outs, (mixed_ref, key_acc, value_acc) = refs[:-3], refs[-3:]
    blocks, _, block, _ = mixed_ref.shape
    key_acc[...] = jnp.zeros_like(key_acc)
    value_acc[...] = jnp.zeros_like(value_acc)

    def tokens(which, first, count):
        return in_ref[pl.ds(first, count), :, which].reshape(count * block, HEAD_DIM)

    def work(i, span):
        low = i - (span - 1)
        width = span * block
        query = tokens(0, i, 1)
        cot = tokens(3, i, 1).astype(jnp.float32)
        key = tokens(1, low, span)
        value = tokens(2, low, span)
        start = start_ref[pl.ds(pl.multiple_of(i * block, block), block), :] - low * block
        col = lax.broadcasted_iota(jnp.int32, (block, width), 1)
        row = lax.broadcasted_iota(jnp.int32, (block, width), 0) + (span - 1) * block
        allowed = (col >= start) & (col <= row)
        score = jnp.where(allowed, dot_nt(query, key), NEG)
        peak = jnp.max(score, axis=1, keepdims=True)
        expo = jnp.exp2((score - peak) * EXP_SCALE)
        inverse = 1.0 / jnp.sum(expo, axis=1, keepdims=True)
        expo_low = expo.astype(jnp.bfloat16)
        mixed = dot_nn(expo_low, value) * inverse
        scaled = cot * inverse
        scaled_low = scaled.astype(jnp.bfloat16)
        rowdot = jnp.sum(mixed * scaled, axis=1, keepdims=True)
        dscore = (expo * (dot_nt(scaled_low, value) - rowdot)).astype(jnp.bfloat16)
        mixed_ref[i, 0] = mixed.astype(jnp.bfloat16)
        mixed_ref[i, 1] = (SCALE * dot_nn(dscore, key)).astype(jnp.bfloat16)
        held = pl.ds(pl.multiple_of(low * block, block), width)
        key_acc[held, :] += dot_tn(dscore, query)
        value_acc[held, :] += dot_tn(expo_low, scaled_low)

    def step(i, carry):
        for span in range(1, spans + 1):
            pl.when(count_ref[i] == span)(functools.partial(work, i, span))
        return carry

    lax.fori_loop(0, blocks, step, 0)
    for d, out_ref in enumerate(outs):
        i = target_ref[d]
        held = pl.ds(pl.multiple_of(i * block, block), block)
        out_ref[:2] = mixed_ref[i]
        out_ref[2] = (SCALE * key_acc[held, :]).astype(jnp.bfloat16)
        out_ref[3] = value_acc[held, :].astype(jnp.bfloat16)


def attention(count, start, targets, packed):
    shards, chans, _, rows, _ = packed.shape
    block = chans * rows
    total = shards * block
    spans = min(shards, (DOC_MAX + block - 2) // block + 1)
    pairs = total * block * min(spans, 3)
    return pl.pallas_call(
        functools.partial(attention_kernel, spans),
        out_shape=[low_array(4, block, HEAD_DIM)] * shards,
        in_specs=[SCALARS, VECTORS, SCALARS, VECTORS],
        out_specs=[VECTORS] * shards,
        scratch_shapes=[
            pltpu.VMEM((shards, 2, block, HEAD_DIM), jnp.bfloat16),
            pltpu.VMEM((total, HEAD_DIM), jnp.float32),
            pltpu.VMEM((total, HEAD_DIM), jnp.float32),
        ],
        compiler_params=pltpu.CompilerParams(vmem_limit_bytes=(10 << 20) + 3072 * total),
        cost_estimate=pl.CostEstimate(
            flops=12 * HEAD_DIM * pairs, bytes_accessed=16 * total * HEAD_DIM, transcendentals=pairs
        ),
    )(count, start, targets, packed)


def unpack_kernel(peers, base, shard_ref, *refs):
    blocks, outs, sems = refs[: len(peers)], refs[-5:-1], refs[-1]
    moves = []
    for b, d in enumerate(peers):
        head = base + jnp.bitwise_xor(shard_ref[0], d)
        columns = pl.ds(pl.multiple_of(head * HEAD_DIM, HEAD_DIM), HEAD_DIM)
        for which in range(4):
            moves.append(
                pltpu.make_async_copy(
                    blocks[b].at[which], outs[which].at[:, columns], sems.at[b, which]
                )
            )
    for move in moves:
        move.start()
    for move in moves:
        move.wait()


def unpack(shard, blocks, peers, base, width, held):
    count = len(blocks)
    rows = blocks[0].shape[1]
    return pl.pallas_call(
        functools.partial(unpack_kernel, peers, base),
        out_shape=[low_array(rows, width)] * 4,
        in_specs=[SCALARS] + [VECTORS] * count + [ANYWHERE] * len(held),
        out_specs=[ANYWHERE] * 4,
        scratch_shapes=[pltpu.SemaphoreType.DMA((count, 4))],
        input_output_aliases={1 + count + i: i for i in range(len(held))},
        compiler_params=pltpu.CompilerParams(vmem_limit_bytes=8 << 20),
        cost_estimate=moved(16 * count * rows * HEAD_DIM),
    )(shard, *blocks, *held)


def exchange(value, d):
    return lax.ppermute(value, "seq", [(s, s ^ d) for s in range(lax.axis_size("seq"))])


def on_device(doc_ids, *inputs):
    shards = lax.axis_size("seq")
    chans = lax.axis_size("chan")
    rows, width = inputs[0].shape
    heads = width // HEAD_DIM // chans
    turns = max(1, heads // shards)
    owners = heads // turns
    copies = shards // owners
    block = rows * chans
    start = jnp.sum((doc_ids[None, :] < doc_ids[:, None]).astype(jnp.int32), axis=1)
    count = jnp.arange(shards, dtype=jnp.int32) - start[::block] // block + 1
    start = start[:, None]
    peers = jnp.bitwise_xor(lax.axis_index("seq"), jnp.arange(shards, dtype=jnp.int32))
    tied = lax.optimization_barrier

    def gather(parts):
        parts = jnp.repeat(parts, copies, axis=0) if copies > 1 else parts
        parts = parts.reshape(shards * chans, 4, rows, HEAD_DIM)
        parts = lax.all_to_all(parts, ("seq", "chan"), split_axis=0, concat_axis=0, tiled=True)
        return parts.reshape(shards, chans, 4, rows, HEAD_DIM)

    parts = [pack(inputs, chans, turns, turn) for turn in range(turns)]
    later, count, start = tied((parts[1:], count, start))
    mine, parts = tied((gather(parts[0]), later))
    order = [0] + sorted(range(1, shards), key=lambda d: (-(d >> 1).bit_count(), d & 1, d))
    outs, blocks = (), ()
    for turn in range(turns):
        following = gather(parts[turn]) if turn + 1 < turns else None
        mine, outs = tied((mine, outs))
        blocks = list(attention(count, start, peers, mine))
        if copies == 1:
            blocks = [exchange(blocks[d], d) if d else blocks[d] for d in order]
            place = lax.axis_index("seq")[None]
        else:
            whole = jnp.stack(blocks)[peers]
            whole = lax.all_to_all(whole, "seq", split_axis=0, concat_axis=0, tiled=True)
            blocks = [whole[owner * copies] for owner in range(owners)]
            place, order = jnp.zeros((1,), jnp.int32), list(range(owners))
        early, base = len(blocks) // 2 + 1, turn * owners
        outs = unpack(place, blocks[:early], order[:early], base, heads * HEAD_DIM, outs)
        outs = unpack(place, blocks[early:], order[early:], base, heads * HEAD_DIM, outs)
        mine = following
    return tuple(outs)


def solution(mesh):
    spread = P(("seq", "chan"), None)
    in_specs = (P(), spread, spread, spread, spread)
    out_specs = (P("seq", "chan"),) * 4
    return jax.shard_map(
        on_device, mesh=mesh, in_specs=in_specs, out_specs=out_specs, check_vma=False
    )
```
